256 devices in a mesh: expert: 64 (over z, x, core), tensor: 4 (over y).
Axes of the slice: x: 4, y: 4, z: 8, core: 2. Of those that a mesh axis runs over, the one named last changes fastest.
Arguments:
- tokens: bfloat16 [2048, 7168], P('expert'), may hold values from -6 to 6
- routes: int32 [2048, 8], P('expert'), may hold values from 0 to 63, all different within a row; in each aligned block of 32 rows (0 to 31, 32 to 63, ...) at most 8 rows name the same one
- gate_weight: bfloat16 [64, 7168, 1024], P('expert', None, 'tensor'), may hold values from -0.0625 to 0.0625
- up_weight: bfloat16 [64, 7168, 1024], P('expert', None, 'tensor'), may hold values from -0.0625 to 0.0625
- down_weight: bfloat16 [64, 1024, 3584], P('expert', 'tensor'), may hold values from -6 to 6
- removed: int32 [64, 256], P('expert'), may hold values from 0 to 1023, as said below
Outputs:
- pruned_down: bfloat16 [64, 1024, 3584], P('expert', 'tensor')
The draws below stay inside these ranges and needn't reach their ends.
Inputs may be any that keep to these rules, and one draw needn't show every extreme that they name: `routes`: among the rows of one index of expert no expert is named more than 8 times, a bound that some block reaches. `removed`: each row holds 256 different hidden units.
All inputs are finite; a program needn't handle non-finite values.
Results may differ from the reference program's by a relative error of at most 0.005.
Values may be sent and summed in bfloat16 or wider, within the bound.
A program may use at most 128 MiB of HBM per device.

```python
import math
import jax
import jax.numpy as jnp
import numpy as np
from jax import lax

D = 7168
FF = 1024
DW = 3584
TOP = 8
K = 256
TOK_DEV = 32
EXPERTS = 64
TOKENS = 2048
MOST = 8


def draw_tokens(key, part):
    key = jax.random.fold_in(key, 11)
    key_common, key_amount, key_noise = jax.random.split(key, 3)
    amount = jax.random.uniform(key_amount, (TOKENS, 1), minval=0.5, maxval=1.5)
    common = jnp.clip(jax.random.normal(key_common, (D,)), -3.5, 3.5)
    noise = 0.3 * jax.random.normal(key_noise, (TOKENS, D))
    values = amount * common[None, :] + noise
    return jnp.clip(values, -6.0, 6.0).astype(jnp.bfloat16)


def draw_removed(key, part):
    key = jax.random.fold_in(key, 7)
    keys = jax.random.split(key, EXPERTS)
    return jax.vmap(lambda single: jax.random.permutation(single, FF)[:K])(keys).astype(jnp.int32)


def block_levels(stream_key, dims, shards, least, largest):
    def one(dim, shards_of):
        steps = jax.random.uniform(jax.random.fold_in(jax.random.fold_in(stream_key, 6), dim), (shards_of,), jnp.float32, least / len(shards), largest / len(shards))
        return jnp.repeat(jnp.exp(steps), dims[dim] // shards_of).reshape((-1,) + (1,) * (len(dims) - dim - 1))

    gain = one(*shards[0])
    for cut in shards[1:]:
        gain = gain * one(*cut)
    return gain


def assign_block(key, own, number, rows, count, top, bound, slope):
    order = jax.random.permutation(key, count)
    heavy_load, ordinary = shares(count, rows * top, bound, slope, True), shares(count, rows * top, bound, slope, False)
    places = jnp.arange(count)

    def named(tallies, offset_by):
        used = int((tallies > 0).sum())
        fixed = max(1, used // 4)
        shifted = fixed + (places - fixed + offset_by * (used - fixed)) % max(1, count - fixed)
        return jnp.zeros((count,), jnp.int32).at[order[jnp.where(places < fixed, places, shifted)]].set(jnp.asarray(tallies, jnp.int32))

    tallies = jnp.where(number % 4 == 0, named(heavy_load, number // 4), named(ordinary, number - number // 4 - 1))
    mixed = jax.random.permutation(jax.random.fold_in(own, 3), count)
    donor, taker = mixed[0:count // 2 * 2:2], mixed[1:count // 2 * 2:2]
    slack = jnp.minimum(tallies[donor] - 1, bound - tallies[taker]) // 2
    slack = jnp.where((donor == order[0]) | (taker == order[0]) | (tallies[taker] == 0), 0, jnp.maximum(slack, 0))
    shifted = jax.random.randint(jax.random.fold_in(own, 4), (count // 2,), 0, 1 << 20) % (slack + 1)
    tallies = tallies.at[donor].add(-shifted).at[taker].add(shifted)
    items = jnp.searchsorted(jnp.cumsum(tallies), jnp.arange(rows * top), side="right").astype(jnp.int32)
    grid = items.reshape(top, rows).T
    grid = grid[jax.random.permutation(jax.random.fold_in(own, 1), rows)]
    offset_by = jax.random.randint(jax.random.fold_in(own, 2), (rows, 1), 0, top)
    return jnp.take_along_axis(grid, (jnp.arange(top)[None, :] + offset_by) % top, axis=1)


def shares(count, total, bound, skew, full):
    loads = [(1 << 20) // math.isqrt(grade ** skew) + 1 for grade in range(1, count + 1)]
    largest = bound if full else min(bound, max(-(-total // count), total * loads[0] // sum(loads)))
    least = 1 if total - largest >= count - 1 else 0
    holding, rest = [largest] + [least] * (count - 1), total - largest - least * (count - 1)
    while rest > 0:
        movable = [i for i in range(1, count) if holding[i] < largest] or [i for i in range(1, count) if holding[i] < bound]
        pool, remaining = sum([loads[i] for i in movable]), rest
        for i in movable:
            extra = min(bound - holding[i], max(1, remaining * loads[i] // pool), rest)
            holding[i] = holding[i] + extra
            rest = rest - extra
    return np.array(holding)


def gaussian(own_key, shape, deviation, reach, cuts=(), kind=jnp.bfloat16):
    drawn = deviation * jax.random.normal(own_key, shape, jnp.float32)
    if cuts:
        drawn = drawn * block_levels(own_key, shape, cuts, -0.22, 0.18)
    return jnp.clip(drawn, -reach, reach).astype(kind)


def setup_inputs(seed: int = 0) -> dict:
    arg_keys = jax.random.split(jax.random.key(seed), 7)
    tokens = draw_tokens(jax.random.fold_in(arg_keys[6], 71), 0)
    routes_keys = jax.random.split(jax.random.fold_in(arg_keys[1], 1), TOKENS // TOK_DEV)
    routes_turns = jax.random.permutation(jax.random.fold_in(arg_keys[1], 3), TOKENS // TOK_DEV)
    routes = jax.vmap(lambda own, number: assign_block(jax.random.fold_in(arg_keys[1], 2), own, number, TOK_DEV, EXPERTS, TOP, MOST, 2))(routes_keys, routes_turns).reshape((TOKENS, TOP))
    gate_weight = gaussian(arg_keys[2], (EXPERTS, D, FF), D ** -0.5, 0.0625, ((0, 64), (2, 4)))
    up_weight = gaussian(arg_keys[3], (EXPERTS, D, FF), D ** -0.5, 0.0625, ((0, 64), (2, 4)))
    down_weight = gaussian(arg_keys[4], (EXPERTS, FF, DW), 1.0, 6.0, ((0, 64), (1, 4)))
    removed = draw_removed(jax.random.fold_in(arg_keys[6], 71), 0)
    return dict(tokens=tokens, routes=routes, gate_weight=gate_weight, up_weight=up_weight, down_weight=down_weight, removed=removed)


def reference(tokens, routes, gate_weight, up_weight, down_weight, removed):
    capacity = min(TOKENS, EXPERTS * MOST)

    def one_expert(pack):
        index, gate_w, up_w, down_w, chosen = pack
        member = jnp.any(routes == index, axis=1).astype(jnp.int32)
        order = jnp.argsort(1 - member, stable=True)[:capacity].astype(jnp.int32)
        rows = tokens[order] * member[order][:, None].astype(tokens.dtype)
        gate = jnp.dot(rows.astype(jnp.float32), gate_w.astype(jnp.float32), preferred_element_type=jnp.float32)
        up = jnp.dot(rows.astype(jnp.float32), up_w.astype(jnp.float32), preferred_element_type=jnp.float32)
        hidden = (jax.nn.silu(gate) * up).astype(jnp.bfloat16)
        gram = jnp.dot(hidden.T.astype(jnp.float32), hidden.astype(jnp.float32), preferred_element_type=jnp.float32)
        shift = 0.1 * jnp.mean(jnp.diagonal(gram)) + 1e-06
        damped = gram + shift * jnp.eye(FF, dtype=jnp.float32)
        lower = jnp.linalg.cholesky(damped)
        picks = (jnp.arange(FF, dtype=jnp.int32)[:, None] == chosen[None, :]).astype(jnp.float32)
        columns = jax.scipy.linalg.cho_solve((lower, True), picks)
        block = jnp.take(columns, chosen, axis=0)
        block = 0.5 * (block + block.T)
        inner = jnp.linalg.cholesky(block)
        mixing = jax.scipy.linalg.cho_solve((inner, True), columns.T).T
        dropped = jnp.dot(picks.T.astype(jnp.bfloat16).astype(jnp.float32), down_w.astype(jnp.float32), preferred_element_type=jnp.float32)
        fixed_rows = down_w.astype(jnp.float32) - jnp.dot(mixing, dropped, precision=lax.Precision.HIGHEST)
        keep = 1.0 - jnp.sum(picks, axis=1, keepdims=True)
        return (fixed_rows * keep).astype(jnp.bfloat16)
    indices = jnp.arange(EXPERTS, dtype=jnp.int32)
    return lax.map(one_expert, (indices, gate_weight, up_weight, down_weight, removed))
```

```python
import functools

import jax
import jax.numpy as jnp
from jax import lax
from jax.experimental import pallas as pl
from jax.experimental.pallas import tpu as pltpu
from jax.sharding import PartitionSpec as P

DAMPING = 0.1
F32 = jnp.float32
BF16 = jnp.bfloat16
SINGLE = 2
ROUNDS = 9
CAP = 1.85


def placing_matrix(routes, experts, capacity):
    tok_rows, top = routes.shape
    flat = routes.reshape(-1)
    onehot = (flat[:, None] == jnp.arange(experts, dtype=jnp.int32)[None, :]).astype(jnp.int32)
    before = jnp.cumsum(onehot, axis=0) - onehot
    slot_in = jnp.sum(before * onehot, axis=1)
    target = (flat * capacity + slot_in).reshape(tok_rows, top)
    slots = jnp.arange(experts * capacity, dtype=jnp.int32)
    hits = target[None, :, :] == slots[:, None, None]
    return jnp.sum(hits.astype(F32), axis=2).astype(BF16)


def dot(a, b, left=1, right=0):
    return lax.dot_general(a, b, (((left,), (right,)), ((), ())), preferred_element_type=F32)


def split(x):
    high = x.astype(BF16)
    return high, (x - high.astype(F32)).astype(BF16)


def three(ah, al, bh, bl):
    return dot(ah, bh) + dot(ah, bl) + dot(al, bh)


def scales(lowest, rounds):
    out = []
    for _ in range(rounds):
        scale = min(2.0 / (1.0 + lowest), CAP)
        out.append(scale)
        lowest = 1.0 - (1.0 - scale * lowest) ** 2
    return out


def solve_kernel(every_ref, chosen_ref, mix_ref):
    parts, rows, own = every_ref.shape
    count = chosen_ref.shape[1]
    order = parts * own
    chosen = chosen_ref[...]
    total = jnp.zeros((1, 1), F32)
    removed = jnp.zeros((rows, count), F32)
    gram = jnp.zeros((rows, rows), F32)
    for part in range(parts):
        block = every_ref[part].astype(F32)
        total = total + jnp.sum(block * block, keepdims=True)
        units = lax.broadcasted_iota(jnp.int32, (own, count), 0) + part * own
        picks = (units == chosen).astype(F32).astype(BF16)
        removed = removed + dot(every_ref[part], picks)
        gone = dot(jnp.ones((8, count), BF16), picks, 1, 1)[:1]
        kept = (block * (1.0 - gone)).astype(BF16)
        gram = gram + dot(kept, kept, 1, 1)
    shift = total * (DAMPING / order) + 1e-6
    bound = total + shift
    inverse_bound = 1.0 / bound
    eye = (
        lax.broadcasted_iota(jnp.int32, (rows, rows), 0)
        == lax.broadcasted_iota(jnp.int32, (rows, rows), 1)
    ).astype(F32)
    gram = (gram + shift * eye) * inverse_bound
    lowest = 0.99 * (DAMPING / order) / (1.0 + DAMPING / order)
    steps = scales(lowest, ROUNDS)
    gh, gl = split(gram)
    x = 2.0 * steps[0] * eye - steps[0] ** 2 * gram
    for k in range(1, ROUNDS):
        scale = steps[k]
        if k <= SINGLE:
            xh = x.astype(BF16)
            z = dot(xh, dot(gh, xh).astype(BF16))
        else:
            xh, xl = split(x)
            yh, yl = split(three(gh, gl, xh, xl))
            z = three(xh, xl, yh, yl)
        x = 2.0 * scale * x - scale ** 2 * z
    xh, xl = split(x)
    rh = removed.astype(BF16)
    w = dot(xh, rh) + dot(xl, rh)
    wh, wl = split(w)
    rest = (removed - three(gh, gl, wh, wl)).astype(BF16)
    w = (w + dot(xh, rest)) * inverse_bound
    wh, wl = split(w)
    me = lax.axis_index("tensor")
    mine = every_ref[me]
    units = lax.broadcasted_iota(jnp.int32, (own, count), 0) + me * own
    keep = 1.0 - jnp.sum((units == chosen).astype(F32), axis=1, keepdims=True)
    mixing = (dot(mine, wh, 0, 0) + dot(mine, wl, 0, 0)) * keep
    high, low = split(mixing)
    mix_ref[0] = high
    mix_ref[1] = low


def solve(every, chosen):
    own = every.shape[2]
    whole = pl.BlockSpec(memory_space=pltpu.VMEM)
    return pl.pallas_call(
        solve_kernel,
        out_shape=jax.ShapeDtypeStruct((2, own, chosen.shape[1]), BF16),
        in_specs=[whole, whole],
        out_specs=whole,
        compiler_params=pltpu.CompilerParams(vmem_limit_bytes=48 * 2**20),
    )(every, chosen)


def final_kernel(mix_ref, chosen_ref, down_ref, dropped_ref, out_ref):
    own, count = mix_ref.shape[1:]
    units = lax.broadcasted_iota(jnp.int32, (own, count), 0) + lax.axis_index("tensor") * own
    keep = 1.0 - jnp.sum((units == chosen_ref[...]).astype(F32), axis=1, keepdims=True)
    dropped = dropped_ref[...]
    change = dot(mix_ref[0], dropped) + dot(mix_ref[1], dropped)
    out_ref[...] = ((down_ref[...].astype(F32) + change) * keep).astype(BF16)


def finish(mix, chosen, down, dropped):
    own, width = down.shape
    count = dropped.shape[0]
    tile = 512 if width % 512 == 0 else width
    return pl.pallas_call(
        final_kernel,
        grid=(width // tile,),
        out_shape=jax.ShapeDtypeStruct((own, width), BF16),
        in_specs=[
            pl.BlockSpec(mix.shape, lambda i: (0, 0, 0)),
            pl.BlockSpec(chosen.shape, lambda i: (0, 0)),
            pl.BlockSpec((own, tile), lambda i: (0, i)),
            pl.BlockSpec((count, tile), lambda i: (0, i)),
        ],
        out_specs=pl.BlockSpec((own, tile), lambda i: (0, i)),
    )(mix, chosen, down, dropped)


def local(tokens, routes, gate_weight, up_weight, down_weight, removed):
    groups = lax.axis_size("expert")
    parts = lax.axis_size("tensor")
    me = lax.axis_index("tensor")
    experts = groups * gate_weight.shape[0]
    tok_rows, width = tokens.shape
    top = routes.shape[1]
    capacity = min(tok_rows, max(2, 2 * tok_rows * top // experts))
    down = down_weight[0]
    own_rows = down.shape[0]
    chosen = removed
    units = jnp.arange(own_rows, dtype=jnp.int32)[:, None] + me * own_rows
    own_picks = (units == chosen).astype(BF16)
    term = jnp.dot(own_picks.T, down, preferred_element_type=F32)
    dropped = lax.psum(term.astype(BF16), "tensor")

    placing = placing_matrix(routes, experts, capacity)
    share = width // parts
    mine = lax.dynamic_slice_in_dim(tokens, me * share, share, 1)
    outgoing = jnp.dot(placing, mine, preferred_element_type=F32).astype(BF16)
    outgoing = outgoing.reshape(experts, capacity, share)
    arrived = lax.all_to_all(outgoing, "expert", split_axis=0, concat_axis=0, tiled=True)
    pieces = lax.all_gather(arrived.reshape(experts * capacity, share), "tensor", axis=0)
    gate = jnp.zeros((experts * capacity, own_rows), F32)
    up = gate
    for part in range(parts):
        at = slice(part * share, (part + 1) * share)
        gate = gate + jnp.dot(pieces[part], gate_weight[0, at], preferred_element_type=F32)
        up = up + jnp.dot(pieces[part], up_weight[0, at], preferred_element_type=F32)
    hidden = (jax.nn.silu(gate) * up).astype(BF16)
    every = lax.all_gather(hidden, "tensor", axis=0)
    mix = solve(every, chosen)
    return finish(mix, chosen, down, dropped)[None]


def solution(mesh):
    in_specs = (
        P("expert", None),
        P("expert", None),
        P("expert", None, "tensor"),
        P("expert", None, "tensor"),
        P("expert", "tensor", None),
        P("expert", None),
    )
    out_specs = P("expert", "tensor", None)
    return jax.shard_map(local, mesh=mesh, in_specs=in_specs, out_specs=out_specs, check_vma=False)
```

```python
import jax
import jax.numpy as jnp
from jax import lax
from jax.experimental import pallas as pl
from jax.experimental.pallas import tpu as pltpu
from jax.sharding import PartitionSpec as P

DAMPING = 0.1
F32 = jnp.float32
BF16 = jnp.bfloat16
SINGLE = 2
ROUNDS = 9
CAP = 1.85


def dot(a, b, left=1, right=0):
    return lax.dot_general(a, b, (((left,), (right,)), ((), ())), preferred_element_type=F32)


def split(x):
    high = x.astype(BF16)
    return high, (x - high.astype(F32)).astype(BF16)


def three(ah, al, bh, bl):
    return dot(ah, bh) + dot(ah, bl) + dot(al, bh)


def scales(lowest, rounds):
    out = []
    for _ in range(rounds):
        scale = min(2.0 / (1.0 + lowest), CAP)
        out.append(scale)
        lowest = 1.0 - (1.0 - scale * lowest) ** 2
    return out


def solve_kernel(every_ref, chosen_ref, mix_ref):
    parts, rows, own = every_ref.shape
    count = chosen_ref.shape[1]
    order = parts * own
    chosen = chosen_ref[...]
    total = jnp.zeros((1, 1), F32)
    removed = jnp.zeros((rows, count), F32)
    gram = jnp.zeros((rows, rows), F32)
    for part in range(parts):
        block = every_ref[part].astype(F32)
        total = total + jnp.sum(block * block, keepdims=True)
        units = lax.broadcasted_iota(jnp.int32, (own, count), 0) + part * own
        picks = (units == chosen).astype(F32).astype(BF16)
        removed = removed + dot(every_ref[part], picks)
        gone = dot(jnp.ones((8, count), BF16), picks, 1, 1)[:1]
        kept = (block * (1.0 - gone)).astype(BF16)
        gram = gram + dot(kept, kept, 1, 1)
    shift = total * (DAMPING / order) + 1e-6
    bound = total + shift
    inverse_bound = 1.0 / bound
    eye = (
        lax.broadcasted_iota(jnp.int32, (rows, rows), 0)
        == lax.broadcasted_iota(jnp.int32, (rows, rows), 1)
    ).astype(F32)
    gram = (gram + shift * eye) * inverse_bound
    lowest = 0.99 * (DAMPING / order) / (1.0 + DAMPING / order)
    steps = scales(lowest, ROUNDS)
    gh, gl = split(gram)
    x = 2.0 * steps[0] * eye - steps[0] ** 2 * gram
    for k in range(1, ROUNDS):
        scale = steps[k]
        if k <= SINGLE:
            xh = x.astype(BF16)
            z = dot(xh, dot(gh, xh).astype(BF16))
        else:
            xh, xl = split(x)
            yh, yl = split(three(gh, gl, xh, xl))
            z = three(xh, xl, yh, yl)
        x = 2.0 * scale * x - scale ** 2 * z
    xh, xl = split(x)
    rh = removed.astype(BF16)
    w = dot(xh, rh) + dot(xl, rh)
    wh, wl = split(w)
    rest = (removed - three(gh, gl, wh, wl)).astype(BF16)
    w = (w + dot(xh, rest)) * inverse_bound
    wh, wl = split(w)
    me = lax.axis_index("tensor")
    mine = every_ref[me]
    units = lax.broadcasted_iota(jnp.int32, (own, count), 0) + me * own
    keep = 1.0 - jnp.sum((units == chosen).astype(F32), axis=1, keepdims=True)
    mixing = (dot(mine, wh, 0, 0) + dot(mine, wl, 0, 0)) * keep
    high, low = split(mixing)
    mix_ref[0] = high
    mix_ref[1] = low


def solve(every, chosen):
    own = every.shape[2]
    whole = pl.BlockSpec(memory_space=pltpu.VMEM)
    return pl.pallas_call(
        solve_kernel,
        out_shape=jax.ShapeDtypeStruct((2, own, chosen.shape[1]), BF16),
        in_specs=[whole, whole],
        out_specs=whole,
        compiler_params=pltpu.CompilerParams(vmem_limit_bytes=48 * 2**20),
    )(every, chosen)


def final_kernel(mix_ref, chosen_ref, down_ref, dropped_ref, out_ref):
    own, count = mix_ref.shape[1:]
    units = lax.broadcasted_iota(jnp.int32, (own, count), 0) + lax.axis_index("tensor") * own
    keep = 1.0 - jnp.sum((units == chosen_ref[...]).astype(F32), axis=1, keepdims=True)
    dropped = dropped_ref[...]
    change = dot(mix_ref[0], dropped) + dot(mix_ref[1], dropped)
    out_ref[...] = ((down_ref[...].astype(F32) + change) * keep).astype(BF16)


def finish(mix, chosen, down, dropped):
    own, width = down.shape
    count = dropped.shape[0]
    tile = 512 if width % 512 == 0 else width
    return pl.pallas_call(
        final_kernel,
        grid=(width // tile,),
        out_shape=jax.ShapeDtypeStruct((own, width), BF16),
        in_specs=[
            pl.BlockSpec(mix.shape, lambda i: (0, 0, 0)),
            pl.BlockSpec(chosen.shape, lambda i: (0, 0)),
            pl.BlockSpec((own, tile), lambda i: (0, i)),
            pl.BlockSpec((count, tile), lambda i: (0, i)),
        ],
        out_specs=pl.BlockSpec((own, tile), lambda i: (0, i)),
    )(mix, chosen, down, dropped)


ZS, XS = 8, 4
CHIPS = ZS * XS
CORES = 2
MOST = 8
MESH = pl.DeviceIdType.MESH


def ring_place(cycle, z, x):
    if cycle == 0:
        return 4 * z + lax.rem(x + z, 4)
    t = lax.rem(z + 5 * x, 8)
    return 4 * (x + 4 * (t // 4)) + lax.rem(t, 4)


def ring_chip(cycle, place):
    if cycle == 0:
        z = place // 4
        x = lax.rem(lax.rem(place, 4) + 3 * z, 4)
    else:
        r = place // 4
        x = lax.rem(r, 4)
        z = lax.rem(3 * r + lax.rem(place, 4), 8)
    return z * XS + x


def dispatch_kernel(
    tok_ref, route_ref, gate_ref, up_ref, every_ref,
    held, told, rows, other, gate_w, up_w, gate_sum, up_sum, hidden,
    ring_send, ring_recv, told_send, told_recv, rows_recv, sib_send, y_send, y_sib_send,
    pre_send, pre_recv, local_sem, weight_sem, hid_send, hid_recv,
):
    index = lax.axis_index("expert")
    t = lax.axis_index("tensor")
    core = lax.rem(index, 2)
    chip = index // 2
    z, x = chip // XS, lax.rem(chip, XS)
    half = lax.rem(t, 2)
    mate = chip * 2 + 1 - core
    above, below, across = lax.rem(t + 1, 4), lax.rem(t + 3, 4), lax.rem(t + 2, 4)
    places = [ring_place(c, z, x) for c in range(2)]
    nexts = [ring_chip(c, lax.rem(places[c] + 1, CHIPS)) * 2 + core for c in range(2)]
    prevs = [ring_chip(c, lax.rem(places[c] + CHIPS - 1, CHIPS)) * 2 + core for c in range(2)]
    tok_rows = tok_ref.shape[0]
    wide = held.shape[-1]

    loads = [
        pltpu.make_async_copy(gate_ref.at[0], gate_w, weight_sem.at[0]),
        pltpu.make_async_copy(up_ref.at[0], up_w, weight_sem.at[1]),
    ]
    for load in loads:
        load.start()

    barrier = pltpu.get_barrier_semaphore()
    partners = [(n, t) for n in nexts + prevs] + [(mate, t)]
    partners += [(e, y) for e in (index, mate) for y in (above, below)] + [(index, across)]
    for partner in partners:
        pl.semaphore_signal(barrier, inc=1, device_id=partner, device_id_type=MESH)
    pl.semaphore_wait(barrier, len(partners))

    def remote(src, dst, send, recv, to):
        return pltpu.make_async_remote_copy(
            src_ref=src, dst_ref=dst, send_sem=send, recv_sem=recv, device_id=to, device_id_type=MESH
        )

    def columns(of_core, cycle):
        first = half * (4 * wide) + of_core * (2 * wide) + cycle * wide
        return pl.ds(pl.multiple_of(first, 128), wide)

    band = pl.ds(pl.multiple_of(core * tok_rows, 32), tok_rows)
    first = []
    for c in range(2):
        first.append(
            remote(
                tok_ref.at[:, columns(1 - core, c)], held.at[c, places[c], band],
                pre_send.at[c], pre_recv.at[c], (mate, t),
            )
        )
        first.append(
            remote(
                route_ref, told.at[c, places[c], core],
                pre_send.at[2 + c], pre_recv.at[2 + c], (mate, t),
            )
        )
    for copy in first:
        copy.start()
    own = []
    for c in range(2):
        own.append(
            pltpu.make_async_copy(
                tok_ref.at[:, columns(core, c)], held.at[c, places[c], band], local_sem.at[c]
            )
        )
        own.append(
            pltpu.make_async_copy(route_ref, told.at[c, places[c], core], local_sem.at[2 + c])
        )
    for copy in own:
        copy.start()
    for copy in own:
        copy.wait()
    for copy in first:
        copy.wait()

    def place_at(c, way, step):
        if way == 0:
            return lax.rem(places[c] + CHIPS - step, CHIPS)
        return lax.rem(places[c] + step, CHIPS)

    def send(c, way, step):
        at = place_at(c, way, step)
        to = ((nexts if way == 0 else prevs)[c], t)
        remote(
            held.at[c, at], held.at[c, at], ring_send.at[c, way], ring_recv.at[c, way, step + 1], to
        ).start()
        remote(
            told.at[c, at], told.at[c, at], told_send.at[c, way], told_recv.at[c, way, step + 1], to
        ).start()

    def take(c, way, step):
        at = place_at(c, way, step)
        to = ((nexts if way == 0 else prevs)[c], t)
        remote(
            held.at[c, at], held.at[c, at], ring_send.at[c, way], ring_recv.at[c, way, step], to
        ).wait_recv()
        remote(
            told.at[c, at], told.at[c, at], told_send.at[c, way], told_recv.at[c, way, step], to
        ).wait_recv()

    lane = lax.broadcasted_iota(jnp.int32, (128, 128), 1)
    earlier = (lax.broadcasted_iota(jnp.int32, (128, 128), 0) < lane).astype(F32).astype(BF16)
    slot = lax.rem(lax.broadcasted_iota(jnp.int32, (4 * MOST, 128), 0), MOST).astype(F32)

    def pick(events):
        marks = []
        for c, at in events:
            for expert in (index, mate):
                for h in range(CORES):
                    named = (told[c, at, h] == expert).astype(F32)
                    marks.append(jnp.broadcast_to(jnp.sum(named, axis=0, keepdims=True), (MOST, 128)))
        marks = jnp.concatenate(marks, axis=0)
        ranks = dot(marks.astype(BF16), earlier)
        out = []
        for n, (c, at) in enumerate(events):
            part = slice(n * 4 * MOST, (n + 1) * 4 * MOST)
            hits = jnp.where(ranks[part] == slot, marks[part], 0.0)[:, : CORES * tok_rows]
            out.append(dot(hits.astype(BF16), held[c, at]).astype(BF16))
        for (c, at), block in zip(events, out):
            source = ring_chip(c, at)
            rows[half * 4 + core * 2 + c, source] = block[: 2 * MOST]
            other[c, source] = block[2 * MOST :]
        for c, at in events:
            source = ring_chip(c, at)
            piece = half * 4 + core * 2 + c
            y = above if c == 0 else below
            target = rows.at[piece, source]
            got = rows_recv.at[piece]
            remote(other.at[c, source], target, y_sib_send.at[c], got, (mate, y)).start()
            remote(rows.at[piece, source], target, y_send.at[c], got, (index, y)).start()
            remote(other.at[c, source], target, sib_send.at[c], got, (mate, t)).start()

    for c in range(2):
        for way in range(2):
            send(c, way, 0)
    pick([(c, places[c]) for c in range(2)])

    def turn(step, carry):
        for c in range(2):
            for way in range(2):
                take(c, way, step)
                if way == 0:
                    send(c, way, step)
                else:
                    @pl.when(step < CHIPS // 2 - 1)
                    def _():
                        send(c, way, step)
        pick([(c, place_at(c, way, step)) for c in range(2) for way in range(2)])
        return carry

    lax.fori_loop(1, CHIPS // 2, turn, 0)
    for c in range(2):
        take(c, 0, CHIPS // 2)
    pick([(c, place_at(c, 0, CHIPS // 2)) for c in range(2)])

    for load in loads:
        load.wait()
    gate_sum[...] = jnp.zeros_like(gate_sum)
    up_sum[...] = jnp.zeros_like(up_sum)

    def multiply(piece):
        at = pl.ds(pl.multiple_of(piece * wide, 128), wide)
        block = rows[piece].reshape(CHIPS * 2 * MOST, wide)
        gate_sum[...] += dot(block, gate_w[at, :])
        up_sum[...] += dot(block, up_w[at, :])

    def piece_step(n, carry):
        kind, c = n // 2, lax.rem(n, 2)
        near = n < 4
        whose = jnp.where(near, jnp.where(n < 2, core, 1 - core), kind - 2)
        piece = jnp.where(near, half, 1 - half) * 4 + whose * 2 + c

        @pl.when(n >= 2)
        def _():
            remote(
                rows.at[piece], rows.at[piece], sib_send.at[0], rows_recv.at[piece], (mate, t)
            ).wait_recv()

        multiply(piece)
        return carry

    lax.fori_loop(0, 8, piece_step, 0)
    gate = gate_sum[...]
    hidden[t] = (gate / (1.0 + jnp.exp(-gate)) * up_sum[...]).astype(BF16)
    copies = [
        remote(hidden.at[t], hidden.at[t], hid_send.at[n], hid_recv.at[n], (index, y))
        for n, y in enumerate((across, above, below))
    ]
    for copy in copies:
        copy.start()
    for c in range(2):
        for way in range(2):
            count = CHIPS // 2 - way
            gone = held.at[c, pl.ds(0, count)]
            remote(gone, gone, ring_send.at[c, way], ring_recv.at[c, way, 0], (mate, t)).wait_send()
            gone = told.at[c, pl.ds(0, count)]
            remote(gone, gone, told_send.at[c, way], told_recv.at[c, way, 0], (mate, t)).wait_send()
        whole = other.at[c]
        for sem in (sib_send, y_send, y_sib_send):
            remote(whole, whole, sem.at[c], rows_recv.at[0], (mate, t)).wait_send()
    for copy in copies:
        copy.wait()
    every_ref[...] = hidden[...]


def dispatch(tokens, told, gate_weight, up_weight):
    tok_rows, width = tokens.shape
    own = gate_weight.shape[2]
    wide = width // 8
    slots = CHIPS * 2 * MOST
    whole = pl.BlockSpec(memory_space=pltpu.VMEM)
    left = pl.BlockSpec(memory_space=pl.ANY)
    dma = pltpu.SemaphoreType.DMA
    return pl.pallas_call(
        dispatch_kernel,
        out_shape=jax.ShapeDtypeStruct((4, slots, own), BF16),
        in_specs=[whole, whole, left, left],
        out_specs=whole,
        scratch_shapes=[
            pltpu.VMEM((2, CHIPS, CORES * tok_rows, wide), BF16),
            pltpu.VMEM((2, CHIPS, CORES, 8, 128), jnp.int32),
            pltpu.VMEM((8, CHIPS, 2 * MOST, wide), BF16),
            pltpu.VMEM((2, CHIPS, 2 * MOST, wide), BF16),
            pltpu.VMEM((width, own), BF16),
            pltpu.VMEM((width, own), BF16),
            pltpu.VMEM((slots, own), F32),
            pltpu.VMEM((slots, own), F32),
            pltpu.VMEM((4, slots, own), BF16),
            dma((2, 2)), dma((2, 2, 17)), dma((2, 2)), dma((2, 2, 17)), dma((8,)), dma((2,)), dma((2,)),
            dma((2,)), dma((4,)), dma((4,)), dma((4,)), dma((2,)), dma((3,)), dma((3,)),
        ],
        compiler_params=pltpu.CompilerParams(
            collective_id=0, has_side_effects=True, vmem_limit_bytes=48 * 2**20
        ),
        cost_estimate=pl.CostEstimate(
            flops=4 * slots * width * own, bytes_accessed=4 * width * own, transcendentals=slots * own
        ),
    )(tokens, told, gate_weight, up_weight)


def local(tokens, routes, gate_weight, up_weight, down_weight, removed):
    me = lax.axis_index("tensor")
    tok_rows, top = routes.shape
    down = down_weight[0]
    own_rows = down.shape[0]
    chosen = removed
    units = jnp.arange(own_rows, dtype=jnp.int32)[:, None] + me * own_rows
    own_picks = (units == chosen).astype(BF16)
    term = jnp.dot(own_picks.T, down, preferred_element_type=F32)
    dropped = lax.psum(term.astype(BF16), "tensor")
    core = lax.rem(lax.axis_index("expert"), CORES)
    told = lax.dynamic_update_slice(
        jnp.full((top, 128), -1, jnp.int32), routes.T, (0, core * tok_rows)
    )
    every = dispatch(tokens, told, gate_weight, up_weight)
    mix = solve(every, chosen)
    return finish(mix, chosen, down, dropped)[None]


def solution(mesh):
    in_specs = (
        P("expert", None),
        P("expert", None),
        P("expert", None, "tensor"),
        P("expert", None, "tensor"),
        P("expert", "tensor", None),
        P("expert", None),
    )
    out_specs = P("expert", "tensor", None)
    return jax.shard_map(local, mesh=mesh, in_specs=in_specs, out_specs=out_specs, check_vma=False)
```

```python
import jax
import jax.numpy as jnp
from jax import lax
from jax.experimental import pallas as pl
from jax.experimental.pallas import tpu as pltpu
from jax.sharding import PartitionSpec as P

DAMPING = 0.1
F32 = jnp.float32
BF16 = jnp.bfloat16
SINGLE = 2
ROUNDS = 9
CAP = 1.85
TILES = 7


def dot(a, b, left=1, right=0):
    return lax.dot_general(a, b, (((left,), (right,)), ((), ())), preferred_element_type=F32)


def split(x):
    high = x.astype(BF16)
    return high, (x - high.astype(F32)).astype(BF16)


def three(ah, al, bh, bl):
    return dot(ah, bh) + dot(ah, bl) + dot(al, bh)


def scales(lowest, rounds):
    out = []
    for _ in range(rounds):
        scale = min(2.0 / (1.0 + lowest), CAP)
        out.append(scale)
        lowest = 1.0 - (1.0 - scale * lowest) ** 2
    return out


def solve_kernel(
    every_ref, chosen_ref, down_ref, dropped_ref, out_ref, down, dropped, result, load_sem, store_sem
):
    loads = [
        pltpu.make_async_copy(down_ref, down, load_sem.at[0]),
        pltpu.make_async_copy(dropped_ref, dropped, load_sem.at[1]),
    ]
    for copy in loads:
        copy.start()
    parts, rows, own = every_ref.shape
    count = chosen_ref.shape[1]
    order = parts * own
    chosen = chosen_ref[...]
    total = jnp.zeros((1, 1), F32)
    removed = jnp.zeros((rows, count), F32)
    gram = jnp.zeros((rows, rows), F32)
    for part in range(parts):
        block = every_ref[part].astype(F32)
        total = total + jnp.sum(block * block, keepdims=True)
        units = lax.broadcasted_iota(jnp.int32, (own, count), 0) + part * own
        picks = (units == chosen).astype(F32).astype(BF16)
        removed = removed + dot(every_ref[part], picks)
        gone = dot(jnp.ones((8, count), BF16), picks, 1, 1)[:1]
        kept = (block * (1.0 - gone)).astype(BF16)
        gram = gram + dot(kept, kept, 1, 1)
    shift = total * (DAMPING / order) + 1e-6
    bound = total + shift
    inverse_bound = 1.0 / bound
    eye = (
        lax.broadcasted_iota(jnp.int32, (rows, rows), 0)
        == lax.broadcasted_iota(jnp.int32, (rows, rows), 1)
    ).astype(F32)
    gram = (gram + shift * eye) * inverse_bound
    lowest = 0.99 * (DAMPING / order) / (1.0 + DAMPING / order)
    steps = scales(lowest, ROUNDS)
    gh, gl = split(gram)
    x = 2.0 * steps[0] * eye - steps[0] ** 2 * gram
    for k in range(1, ROUNDS):
        scale = steps[k]
        if k <= SINGLE:
            xh = x.astype(BF16)
            z = dot(xh, dot(gh, xh).astype(BF16))
        else:
            xh, xl = split(x)
            yh, yl = split(three(gh, gl, xh, xl))
            z = three(xh, xl, yh, yl)
        x = 2.0 * scale * x - scale ** 2 * z
    xh, xl = split(x)
    rh = removed.astype(BF16)
    w = dot(xh, rh) + dot(xl, rh)
    wh, wl = split(w)
    rest = (removed - three(gh, gl, wh, wl)).astype(BF16)
    w = (w + dot(xh, rest)) * inverse_bound
    wh, wl = split(w)
    me = lax.axis_index("tensor")
    mine = every_ref[me]
    units = lax.broadcasted_iota(jnp.int32, (own, count), 0) + me * own
    keep = 1.0 - jnp.sum((units == chosen).astype(F32), axis=1, keepdims=True)
    mixing = (dot(mine, wh, 0, 0) + dot(mine, wl, 0, 0)) * keep
    high, low = split(mixing)
    for copy in loads:
        copy.wait()
    width = down_ref.shape[1]
    tile = width // TILES
    stores = []
    for n in range(TILES):
        at = slice(n * tile, (n + 1) * tile)
        part = dropped[:, at]
        change = dot(high, part) + dot(low, part)
        result[:, at] = ((down[:, at].astype(F32) + change) * keep).astype(BF16)
        stores.append(pltpu.make_async_copy(result.at[:, at], out_ref.at[:, at], store_sem.at[n]))
        stores[-1].start()
    for copy in stores:
        copy.wait()


def solve(every, chosen, down, dropped):
    own, width = down.shape
    count = chosen.shape[1]
    whole = pl.BlockSpec(memory_space=pltpu.VMEM)
    left = pl.BlockSpec(memory_space=pl.ANY)
    return pl.pallas_call(
        solve_kernel,
        out_shape=jax.ShapeDtypeStruct((own, width), BF16),
        in_specs=[whole, whole, left, left],
        out_specs=left,
        scratch_shapes=[
            pltpu.VMEM((own, width), BF16),
            pltpu.VMEM((count, width), BF16),
            pltpu.VMEM((own, width), BF16),
            pltpu.SemaphoreType.DMA((2,)),
            pltpu.SemaphoreType.DMA((TILES,)),
        ],
        compiler_params=pltpu.CompilerParams(vmem_limit_bytes=48 * 2**20),
    )(every, chosen, down, dropped)


ZS, XS = 8, 4
CHIPS = ZS * XS
CORES = 2
MOST = 8
MESH = pl.DeviceIdType.MESH


def dispatch_kernel(
    tok_ref, route_ref, gate_ref, up_ref, every_ref,
    held, told, rows, other, gate_w, up_w, gate_sum, up_sum, hidden,
    held_send, held_recv, told_send, told_recv, rows_recv, sib_send, y_send, y_sib_send,
    pre_send, pre_recv, local_sem, weight_sem, hid_send, hid_recv,
):
    index = lax.axis_index("expert")
    t = lax.axis_index("tensor")
    core = lax.rem(index, 2)
    chip = index // 2
    z, x = chip // XS, lax.rem(chip, XS)
    half = lax.rem(t, 2)
    mate = chip * 2 + 1 - core
    above, below, across = lax.rem(t + 1, 4), lax.rem(t + 3, 4), lax.rem(t + 2, 4)
    here = chip
    z_up, z_down = (lax.rem(z + 1, ZS) * XS + x) * 2 + core, (lax.rem(z + ZS - 1, ZS) * XS + x) * 2 + core
    x_up, x_down = (z * XS + lax.rem(x + 1, XS)) * 2 + core, (z * XS + lax.rem(x + XS - 1, XS)) * 2 + core
    tok_rows = tok_ref.shape[0]
    wide = held.shape[-1]

    loads = [
        pltpu.make_async_copy(gate_ref.at[0], gate_w, weight_sem.at[0]),
        pltpu.make_async_copy(up_ref.at[0], up_w, weight_sem.at[1]),
    ]
    for load in loads:
        load.start()

    barrier = pltpu.get_barrier_semaphore()
    partners = [(n, t) for n in (z_up, z_down, x_up, x_down)] + [(mate, t)]
    partners += [(e, y) for e in (index, mate) for y in (above, below)] + [(index, across)]
    for partner in partners:
        pl.semaphore_signal(barrier, inc=1, device_id=partner, device_id_type=MESH)
    pl.semaphore_wait(barrier, len(partners))

    def remote(src, dst, send, recv, to):
        return pltpu.make_async_remote_copy(
            src_ref=src, dst_ref=dst, send_sem=send, recv_sem=recv, device_id=to, device_id_type=MESH
        )

    def columns(of_core, cycle):
        first = half * (4 * wide) + of_core * (2 * wide) + cycle * wide
        return pl.ds(pl.multiple_of(first, 128), wide)

    band = pl.ds(pl.multiple_of(core * tok_rows, 32), tok_rows)
    first = []
    for c in range(2):
        first.append(
            remote(
                tok_ref.at[:, columns(1 - core, c)], held.at[c, here, band],
                pre_send.at[c], pre_recv.at[c], (mate, t),
            )
        )
    first.append(
        remote(route_ref, told.at[here, core], pre_send.at[2], pre_recv.at[2], (mate, t))
    )
    for copy in first:
        copy.start()
    own = []
    for c in range(2):
        own.append(
            pltpu.make_async_copy(
                tok_ref.at[:, columns(core, c)], held.at[c, here, band], local_sem.at[c]
            )
        )
    own.append(pltpu.make_async_copy(route_ref, told.at[here, core], local_sem.at[2]))
    for copy in own:
        copy.start()
    for copy in own:
        copy.wait()
    for copy in first:
        copy.wait()

    def at(dz, dx):
        return lax.rem(z + dz + 2 * ZS, ZS) * XS + lax.rem(x + dx + 2 * XS, XS)

    def go(c, block, to):
        remote(
            held.at[c, block], held.at[c, block], held_send.at[c], held_recv.at[c, block], (to, t)
        ).start()
        if c == 0:
            remote(
                told.at[block], told.at[block], told_send.at[0], told_recv.at[block], (to, t)
            ).start()

    def take(c, block):
        remote(
            held.at[c, block], held.at[c, block], held_send.at[c], held_recv.at[c, block], (mate, t)
        ).wait_recv()
        if c == 0:
            remote(
                told.at[block], told.at[block], told_send.at[0], told_recv.at[block], (mate, t)
            ).wait_recv()

    lane = lax.broadcasted_iota(jnp.int32, (128, 128), 1)
    earlier = (lax.broadcasted_iota(jnp.int32, (128, 128), 0) < lane).astype(F32).astype(BF16)
    slot = lax.rem(lax.broadcasted_iota(jnp.int32, (4 * MOST, 128), 0), MOST).astype(F32)

    def pick(events):
        marks = []
        for c, block in events:
            for expert in (index, mate):
                for h in range(CORES):
                    named = (told[block, h] == expert).astype(F32)
                    marks.append(jnp.broadcast_to(jnp.sum(named, axis=0, keepdims=True), (MOST, 128)))
        marks = jnp.concatenate(marks, axis=0)
        ranks = dot(marks.astype(BF16), earlier)
        out = []
        for n, (c, block) in enumerate(events):
            part = slice(n * 4 * MOST, (n + 1) * 4 * MOST)
            hits = jnp.where(ranks[part] == slot, marks[part], 0.0)[:, : CORES * tok_rows]
            out.append(dot(hits.astype(BF16), held[c, block]).astype(BF16))
        for (c, source), picked in zip(events, out):
            rows[half * 4 + core * 2 + c, source] = picked[: 2 * MOST]
            other[c, source] = picked[2 * MOST :]
        for c, source in events:
            piece = half * 4 + core * 2 + c
            y = above if c == 0 else below
            target = rows.at[piece, source]
            got = rows_recv.at[piece]
            remote(other.at[c, source], target, y_sib_send.at[c], got, (mate, y)).start()
            remote(rows.at[piece, source], target, y_send.at[c], got, (index, y)).start()
            remote(other.at[c, source], target, sib_send.at[c], got, (mate, t)).start()

    for c in range(2):
        for to in (z_up, z_down, x_up, x_down):
            go(c, here, to)
    pick([(0, here), (1, here)])

    def turn(r, carry):
        @pl.when(r <= 4)
        def _():
            block = at(-r, 0)
            take(0, block)

            @pl.when(r < 4)
            def _():
                go(0, block, z_up)

            go(0, block, x_up)
            go(0, block, x_down)

        @pl.when(r <= 3)
        def _():
            block = at(r, 0)
            take(0, block)

            @pl.when(r < 3)
            def _():
                go(0, block, z_down)

            go(0, block, x_up)
            go(0, block, x_down)

        @pl.when(r == 1)
        def _():
            block = at(0, -1)
            take(1, block)
            go(1, block, x_up)
            go(1, block, z_up)
            go(1, block, z_down)
            block = at(0, 1)
            take(1, block)
            go(1, block, z_up)
            go(1, block, z_down)

        @pl.when(r == 2)
        def _():
            block = at(0, 2)
            take(1, block)
            go(1, block, z_up)
            go(1, block, z_down)

        for dx in (0, -1, 1, 2):
            hop = r - abs(dx)
            even = lax.rem(x + dx + XS, 2) == 0
            for sign, to, most in ((-1, z_up, jnp.where(even, 4, 3)), (1, z_down, jnp.where(even, 3, 4))):
                @pl.when((hop >= 1) & (hop <= most))
                def _():
                    block = at(sign * hop, dx)
                    take(1, block)

                    @pl.when(hop < most)
                    def _():
                        go(1, block, to)

        for sign in (-1, 1):
            far = r - 1
            there = (far <= 4) if sign < 0 else (far >= 1) & (far <= 3)

            @pl.when(there)
            def _():
                even = lax.rem(z + far, 2) == 0
                block = at(sign * far, -1)
                take(0, block)

                @pl.when(even)
                def _():
                    go(0, block, x_up)

                back = at(sign * far, 1)
                take(0, back)

                @pl.when(jnp.logical_not(even))
                def _():
                    go(0, back, x_down)

        for sign in (-1, 1):
            far = r - 2
            there = (far >= 0) if sign < 0 else (far >= 1) & (far <= 3)

            @pl.when(there)
            def _():
                take(0, at(sign * far, 2))

        for dx in (0, -1, 1, 2):
            far = r - abs(dx)
            for sign in (-1, 1):
                there = (far >= 0) & (far <= 4) if sign < 0 else (far >= 1) & (far <= 3)

                @pl.when(there)
                def _():
                    block = at(sign * far, dx)
                    pick([(0, block), (1, block)])

        return carry

    lax.fori_loop(1, 7, turn, 0)

    for load in loads:
        load.wait()
    gate_sum[...] = jnp.zeros_like(gate_sum)
    up_sum[...] = jnp.zeros_like(up_sum)

    def multiply(piece, first, count):
        cut = pl.ds(pl.multiple_of(piece * wide, 128), wide)
        block = rows[piece, first : first + count].reshape(count * 2 * MOST, wide)
        span = slice(first * 2 * MOST, (first + count) * 2 * MOST)
        gate_sum[span] += dot(block, gate_w[cut, :])
        up_sum[span] += dot(block, up_w[cut, :])

    def arrived(piece):
        remote(
            rows.at[piece], rows.at[piece], sib_send.at[0], rows_recv.at[piece], (mate, t)
        ).wait_recv()

    def near(n, carry):
        piece = half * 4 + jnp.where(n < 2, core, 1 - core) * 2 + lax.rem(n, 2)

        @pl.when(n >= 2)
        def _():
            arrived(piece)

        multiply(piece, 0, CHIPS)
        return carry

    lax.fori_loop(0, 4, near, 0)
    copies = []
    middle = CHIPS // 2
    for part in range(2):
        def far(n, carry):
            piece = (1 - half) * 4 + n
            if part == 0:
                arrived(piece)
            multiply(piece, part * middle, middle)
            return carry

        lax.fori_loop(0, 4, far, 0)
        span = slice(part * middle * 2 * MOST, (part + 1) * middle * 2 * MOST)
        gate = gate_sum[span]
        hidden[t, span] = (gate / (1.0 + jnp.exp(-gate)) * up_sum[span]).astype(BF16)
        for n, y in enumerate((across, above, below)):
            mine = hidden.at[t, span]
            copies.append(
                remote(mine, mine, hid_send.at[part, n], hid_recv.at[part, n], (index, y))
            )
            copies[-1].start()
    gone = told.at[pl.ds(0, CHIPS - 1)]
    remote(gone, gone, told_send.at[0], told_recv.at[0], (mate, t)).wait_send()
    for c in range(2):
        gone = held.at[c, pl.ds(0, CHIPS - 1)]
        remote(gone, gone, held_send.at[c], held_recv.at[c, 0], (mate, t)).wait_send()
        whole = other.at[c]
        for sem in (sib_send, y_send, y_sib_send):
            remote(whole, whole, sem.at[c], rows_recv.at[0], (mate, t)).wait_send()
    for copy in copies:
        copy.wait()
    every_ref[...] = hidden[...]


def dispatch(tokens, told, gate_weight, up_weight):
    tok_rows, width = tokens.shape
    own = gate_weight.shape[2]
    wide = width // 8
    slots = CHIPS * 2 * MOST
    whole = pl.BlockSpec(memory_space=pltpu.VMEM)
    left = pl.BlockSpec(memory_space=pl.ANY)
    dma = pltpu.SemaphoreType.DMA
    return pl.pallas_call(
        dispatch_kernel,
        out_shape=jax.ShapeDtypeStruct((4, slots, own), BF16),
        in_specs=[left, whole, left, left],
        out_specs=whole,
        scratch_shapes=[
            pltpu.VMEM((2, CHIPS, CORES * tok_rows, wide), BF16),
            pltpu.VMEM((CHIPS, CORES, 8, 128), jnp.int32),
            pltpu.VMEM((8, CHIPS, 2 * MOST, wide), BF16),
            pltpu.VMEM((2, CHIPS, 2 * MOST, wide), BF16),
            pltpu.VMEM((width, own), BF16),
            pltpu.VMEM((width, own), BF16),
            pltpu.VMEM((slots, own), F32),
            pltpu.VMEM((slots, own), F32),
            pltpu.VMEM((4, slots, own), BF16),
            dma((2,)), dma((2, CHIPS)), dma((1,)), dma((CHIPS,)), dma((8,)), dma((2,)), dma((2,)),
            dma((2,)), dma((3,)), dma((3,)), dma((3,)), dma((2,)), dma((2, 3)), dma((2, 3)),
        ],
        compiler_params=pltpu.CompilerParams(
            collective_id=0, has_side_effects=True, vmem_limit_bytes=48 * 2**20
        ),
        cost_estimate=pl.CostEstimate(
            flops=4 * slots * width * own, bytes_accessed=4 * width * own, transcendentals=slots * own
        ),
    )(tokens, told, gate_weight, up_weight)


def local(tokens, routes, gate_weight, up_weight, down_weight, removed):
    me = lax.axis_index("tensor")
    tok_rows, top = routes.shape
    down = down_weight[0]
    own_rows = down.shape[0]
    chosen = removed
    units = jnp.arange(own_rows, dtype=jnp.int32)[:, None] + me * own_rows
    own_picks = (units == chosen).astype(BF16)
    term = jnp.dot(own_picks.T, down, preferred_element_type=F32)
    dropped = lax.psum(term.astype(BF16), "tensor")
    core = lax.rem(lax.axis_index("expert"), CORES)
    told = lax.dynamic_update_slice(
        jnp.full((top, 128), -1, jnp.int32), routes.T, (0, core * tok_rows)
    )
    every = dispatch(tokens, told, gate_weight, up_weight)
    return solve(every, chosen, down, dropped)[None]


def solution(mesh):
    in_specs = (
        P("expert", None),
        P("expert", None),
        P("expert", None, "tensor"),
        P("expert", None, "tensor"),
        P("expert", "tensor", None),
        P("expert", None),
    )
    out_specs = P("expert", "tensor", None)
    return jax.shard_map(local, mesh=mesh, in_specs=in_specs, out_specs=out_specs, check_vma=False)
```

```python
import jax
import jax.numpy as jnp
from jax import lax
from jax.experimental import pallas as pl
from jax.experimental.pallas import tpu as pltpu
from jax.sharding import PartitionSpec as P

DAMPING = 0.1
F32 = jnp.float32
BF16 = jnp.bfloat16
MESH = pl.DeviceIdType.MESH
SINGLE = 2
ROUNDS = 9
CAP = 1.85


def dot(a, b, left=1, right=0):
    return lax.dot_general(a, b, (((left,), (right,)), ((), ())), preferred_element_type=F32)


def split(x):
    high = x.astype(BF16)
    return high, (x - high.astype(F32)).astype(BF16)


def three(ah, al, bh, bl):
    return dot(ah, bh) + dot(ah, bl) + dot(al, bh)


def scales(lowest, rounds):
    out = []
    for _ in range(rounds):
        scale = min(2.0 / (1.0 + lowest), CAP)
        out.append(scale)
        lowest = 1.0 - (1.0 - scale * lowest) ** 2
    return out


def solve_kernel(
    every_ref, chosen_ref, down_ref, slice_ref, out_ref,
    down, dropped, result, load_sem, store_sem, send_sem, recv_sem,
):
    index = lax.axis_index("expert")
    me = lax.axis_index("tensor")
    load = pltpu.make_async_copy(down_ref, down, load_sem.at[0])
    load.start()
    others = [lax.rem(me + n, 4) for n in (2, 1, 3)]
    barrier = pltpu.get_barrier_semaphore()
    for y in others:
        pl.semaphore_signal(barrier, inc=1, device_id=(index, y), device_id_type=MESH)
    dropped[me] = slice_ref[...]
    pl.semaphore_wait(barrier, 3)
    copies = [
        pltpu.make_async_remote_copy(
            src_ref=slice_ref, dst_ref=dropped.at[me], send_sem=send_sem.at[n], recv_sem=recv_sem.at[n],
            device_id=(index, y), device_id_type=MESH,
        )
        for n, y in enumerate(others)
    ]
    for copy in copies:
        copy.start()
    parts, rows, own = every_ref.shape
    count = chosen_ref.shape[1]
    order = parts * own
    chosen = chosen_ref[...]
    total = jnp.zeros((1, 1), F32)
    removed = jnp.zeros((rows, count), F32)
    gram = jnp.zeros((rows, rows), F32)
    for part in range(parts):
        block = every_ref[part].astype(F32)
        total = total + jnp.sum(block * block, keepdims=True)
        units = lax.broadcasted_iota(jnp.int32, (own, count), 0) + part * own
        picks = (units == chosen).astype(F32).astype(BF16)
        removed = removed + dot(every_ref[part], picks)
        gone = dot(jnp.ones((8, count), BF16), picks, 1, 1)[:1]
        kept = (block * (1.0 - gone)).astype(BF16)
        gram = gram + dot(kept, kept, 1, 1)
    shift = total * (DAMPING / order) + 1e-6
    bound = total + shift
    inverse_bound = 1.0 / bound
    eye = (
        lax.broadcasted_iota(jnp.int32, (rows, rows), 0)
        == lax.broadcasted_iota(jnp.int32, (rows, rows), 1)
    ).astype(F32)
    gram = (gram + shift * eye) * inverse_bound
    lowest = 0.99 * (DAMPING / order) / (1.0 + DAMPING / order)
    steps = scales(lowest, ROUNDS)
    gh, gl = split(gram)
    x = 2.0 * steps[0] * eye - steps[0] ** 2 * gram
    for k in range(1, ROUNDS):
        scale = steps[k]
        if k <= SINGLE:
            xh = x.astype(BF16)
            z = dot(xh, dot(gh, xh).astype(BF16))
        else:
            xh, xl = split(x)
            yh, yl = split(three(gh, gl, xh, xl))
            z = three(xh, xl, yh, yl)
        x = 2.0 * scale * x - scale ** 2 * z
    xh, xl = split(x)
    rh = removed.astype(BF16)
    w = dot(xh, rh) + dot(xl, rh)
    wh, wl = split(w)
    rest = (removed - three(gh, gl, wh, wl)).astype(BF16)
    w = (w + dot(xh, rest)) * inverse_bound
    wh, wl = split(w)
    mine = every_ref[me]
    units = lax.broadcasted_iota(jnp.int32, (own, count), 0) + me * own
    keep = 1.0 - jnp.sum((units == chosen).astype(F32), axis=1, keepdims=True)
    mixing = (dot(mine, wh, 0, 0) + dot(mine, wl, 0, 0)) * keep
    high, low = split(mixing)
    load.wait()
    for copy in copies:
        copy.wait()
    tile = dropped.shape[2]
    stores = []
    for n in range(4):
        at = slice(n * tile, (n + 1) * tile)
        part = dropped[n]
        change = dot(high, part) + dot(low, part)
        result[:, at] = ((down[:, at].astype(F32) + change) * keep).astype(BF16)
        stores.append(pltpu.make_async_copy(result.at[:, at], out_ref.at[:, at], store_sem.at[n]))
        stores[-1].start()
    for copy in stores:
        copy.wait()


def solve(every, chosen, down, part):
    own, width = down.shape
    count = chosen.shape[1]
    whole = pl.BlockSpec(memory_space=pltpu.VMEM)
    left = pl.BlockSpec(memory_space=pl.ANY)
    return pl.pallas_call(
        solve_kernel,
        out_shape=jax.ShapeDtypeStruct((own, width), BF16),
        in_specs=[whole, whole, left, whole],
        out_specs=left,
        scratch_shapes=[
            pltpu.VMEM((own, width), BF16),
            pltpu.VMEM((4, count, width // 4), BF16),
            pltpu.VMEM((own, width), BF16),
            pltpu.SemaphoreType.DMA((1,)),
            pltpu.SemaphoreType.DMA((4,)),
            pltpu.SemaphoreType.DMA((3,)),
            pltpu.SemaphoreType.DMA((3,)),
        ],
        compiler_params=pltpu.CompilerParams(
            collective_id=1, has_side_effects=True, vmem_limit_bytes=48 * 2**20
        ),
    )(every, chosen, down, part)


ZS, XS = 8, 4
CHIPS = ZS * XS
CORES = 2
MOST = 8


def dispatch_kernel(
    tok_ref, route_ref, gate_ref, up_ref, down_ref, chosen_ref, every_ref, slice_ref,
    held, told, rows, other, gate_w, up_w, gate_sum, up_sum, hidden,
    held_send, held_recv, told_send, told_recv, rows_recv, sib_send, y_send, y_sib_send,
    pre_send, pre_recv, local_sem, weight_sem, hid_send, hid_recv,
    down, term, gained, down_sem, drop_send, drop_recv,
):
    index = lax.axis_index("expert")
    t = lax.axis_index("tensor")
    core = lax.rem(index, 2)
    chip = index // 2
    z, x = chip // XS, lax.rem(chip, XS)
    half = lax.rem(t, 2)
    mate = chip * 2 + 1 - core
    above, below, across = lax.rem(t + 1, 4), lax.rem(t + 3, 4), lax.rem(t + 2, 4)
    here = chip
    z_up, z_down = (lax.rem(z + 1, ZS) * XS + x) * 2 + core, (lax.rem(z + ZS - 1, ZS) * XS + x) * 2 + core
    x_up, x_down = (z * XS + lax.rem(x + 1, XS)) * 2 + core, (z * XS + lax.rem(x + XS - 1, XS)) * 2 + core
    tok_rows = tok_ref.shape[0]
    wide = held.shape[-1]

    loads = [
        pltpu.make_async_copy(gate_ref.at[0], gate_w, weight_sem.at[0]),
        pltpu.make_async_copy(up_ref.at[0], up_w, weight_sem.at[1]),
    ]
    down_load = pltpu.make_async_copy(down_ref, down, down_sem.at[0])
    down_load.start()

    barrier = pltpu.get_barrier_semaphore()
    partners = [(n, t) for n in (z_up, z_down, x_up, x_down)] + [(mate, t)]
    partners += [(e, y) for e in (index, mate) for y in (above, below)] + [(index, across)]
    for partner in partners:
        pl.semaphore_signal(barrier, inc=1, device_id=partner, device_id_type=MESH)
    pl.semaphore_wait(barrier, len(partners))

    def remote(src, dst, send, recv, to):
        return pltpu.make_async_remote_copy(
            src_ref=src, dst_ref=dst, send_sem=send, recv_sem=recv, device_id=to, device_id_type=MESH
        )

    def columns(of_core, cycle):
        first = half * (4 * wide) + of_core * (2 * wide) + cycle * wide
        return pl.ds(pl.multiple_of(first, 128), wide)

    band = pl.ds(pl.multiple_of(core * tok_rows, 32), tok_rows)
    first = []
    for c in range(2):
        first.append(
            remote(
                tok_ref.at[:, columns(1 - core, c)], held.at[c, here, band],
                pre_send.at[c], pre_recv.at[c], (mate, t),
            )
        )
    first.append(
        remote(route_ref, told.at[here, core], pre_send.at[2], pre_recv.at[2], (mate, t))
    )
    for copy in first:
        copy.start()
    own = []
    for c in range(2):
        own.append(
            pltpu.make_async_copy(
                tok_ref.at[:, columns(core, c)], held.at[c, here, band], local_sem.at[c]
            )
        )
    own.append(pltpu.make_async_copy(route_ref, told.at[here, core], local_sem.at[2]))
    for copy in own + loads:
        copy.start()
    for copy in own:
        copy.wait()
    for copy in first:
        copy.wait()

    def at(dz, dx):
        return lax.rem(z + dz + 2 * ZS, ZS) * XS + lax.rem(x + dx + 2 * XS, XS)

    def go(c, block, to):
        remote(
            held.at[c, block], held.at[c, block], held_send.at[c], held_recv.at[c, block], (to, t)
        ).start()
        if c == 0:
            remote(
                told.at[block], told.at[block], told_send.at[0], told_recv.at[block], (to, t)
            ).start()

    def take(c, block):
        remote(
            held.at[c, block], held.at[c, block], held_send.at[c], held_recv.at[c, block], (mate, t)
        ).wait_recv()
        if c == 0:
            remote(
                told.at[block], told.at[block], told_send.at[0], told_recv.at[block], (mate, t)
            ).wait_recv()

    lane = lax.broadcasted_iota(jnp.int32, (128, 128), 1)
    earlier = (lax.broadcasted_iota(jnp.int32, (128, 128), 0) < lane).astype(F32).astype(BF16)
    slot = lax.rem(lax.broadcasted_iota(jnp.int32, (4 * MOST, 128), 0), MOST).astype(F32)

    def pick(events):
        marks = []
        for c, block in events:
            for expert in (index, mate):
                for h in range(CORES):
                    named = (told[block, h] == expert).astype(F32)
                    marks.append(jnp.broadcast_to(jnp.sum(named, axis=0, keepdims=True), (MOST, 128)))
        marks = jnp.concatenate(marks, axis=0)
        ranks = dot(marks.astype(BF16), earlier)
        out = []
        for n, (c, block) in enumerate(events):
            part = slice(n * 4 * MOST, (n + 1) * 4 * MOST)
            hits = jnp.where(ranks[part] == slot, marks[part], 0.0)[:, : CORES * tok_rows]
            out.append(dot(hits.astype(BF16), held[c, block]).astype(BF16))
        for (c, source), picked in zip(events, out):
            rows[half * 4 + core * 2 + c, source] = picked[: 2 * MOST]
            other[c, source] = picked[2 * MOST :]
        for c, source in events:
            piece = half * 4 + core * 2 + c
            y = above if c == 0 else below
            target = rows.at[piece, source]
            got = rows_recv.at[piece]
            remote(other.at[c, source], target, y_sib_send.at[c], got, (mate, y)).start()
            remote(rows.at[piece, source], target, y_send.at[c], got, (index, y)).start()
            remote(other.at[c, source], target, sib_send.at[c], got, (mate, t)).start()

    for c in range(2):
        for to in (z_up, z_down, x_up, x_down):
            go(c, here, to)
    pick([(0, here), (1, here)])

    down_load.wait()
    own_rows, count = down.shape[0], chosen_ref.shape[1]
    units = lax.broadcasted_iota(jnp.int32, (own_rows, count), 0) + t * own_rows
    picks = (units == chosen_ref[...]).astype(F32).astype(BF16)
    share = term.shape[-1]
    for u in range(4):
        term[u] = dot(picks, down[:, u * share : (u + 1) * share], 0, 0).astype(BF16)
    drops = [
        remote(term.at[y], gained.at[n], drop_send.at[n], drop_recv.at[n], (index, y))
        for n, y in enumerate((across, above, below))
    ]
    for copy in drops:
        copy.start()

    def turn(r, carry):
        @pl.when(r <= 4)
        def _():
            block = at(-r, 0)
            take(0, block)

            @pl.when(r < 4)
            def _():
                go(0, block, z_up)

            go(0, block, x_up)
            go(0, block, x_down)

        @pl.when(r <= 3)
        def _():
            block = at(r, 0)
            take(0, block)

            @pl.when(r < 3)
            def _():
                go(0, block, z_down)

            go(0, block, x_up)
            go(0, block, x_down)

        @pl.when(r == 1)
        def _():
            block = at(0, -1)
            take(1, block)
            go(1, block, x_up)
            go(1, block, z_up)
            go(1, block, z_down)
            block = at(0, 1)
            take(1, block)
            go(1, block, z_up)
            go(1, block, z_down)

        @pl.when(r == 2)
        def _():
            block = at(0, 2)
            take(1, block)
            go(1, block, z_up)
            go(1, block, z_down)

        for dx in (0, -1, 1, 2):
            hop = r - abs(dx)
            even = lax.rem(x + dx + XS, 2) == 0
            for sign, to, most in ((-1, z_up, jnp.where(even, 4, 3)), (1, z_down, jnp.where(even, 3, 4))):
                @pl.when((hop >= 1) & (hop <= most))
                def _():
                    block = at(sign * hop, dx)
                    take(1, block)

                    @pl.when(hop < most)
                    def _():
                        go(1, block, to)

        for sign in (-1, 1):
            far = r - 1
            there = (far <= 4) if sign < 0 else (far >= 1) & (far <= 3)

            @pl.when(there)
            def _():
                even = lax.rem(z + far, 2) == 0
                block = at(sign * far, -1)
                take(0, block)

                @pl.when(even)
                def _():
                    go(0, block, x_up)

                back = at(sign * far, 1)
                take(0, back)

                @pl.when(jnp.logical_not(even))
                def _():
                    go(0, back, x_down)

        for sign in (-1, 1):
            far = r - 2
            there = (far >= 0) if sign < 0 else (far >= 1) & (far <= 3)

            @pl.when(there)
            def _():
                take(0, at(sign * far, 2))

        for dx in (0, -1, 1, 2):
            far = r - abs(dx)
            for sign in (-1, 1):
                there = (far >= 0) & (far <= 4) if sign < 0 else (far >= 1) & (far <= 3)

                @pl.when(there)
                def _():
                    block = at(sign * far, dx)
                    pick([(0, block), (1, block)])

        return carry

    lax.fori_loop(1, 7, turn, 0)

    for load in loads:
        load.wait()
    gate_sum[...] = jnp.zeros_like(gate_sum)
    up_sum[...] = jnp.zeros_like(up_sum)

    def multiply(piece, first, count):
        cut = pl.ds(pl.multiple_of(piece * wide, 128), wide)
        block = rows[piece, first : first + count].reshape(count * 2 * MOST, wide)
        span = slice(first * 2 * MOST, (first + count) * 2 * MOST)
        gate_sum[span] += dot(block, gate_w[cut, :])
        up_sum[span] += dot(block, up_w[cut, :])

    def arrived(piece):
        remote(
            rows.at[piece], rows.at[piece], sib_send.at[0], rows_recv.at[piece], (mate, t)
        ).wait_recv()

    def near(n, carry):
        piece = half * 4 + jnp.where(n < 2, core, 1 - core) * 2 + lax.rem(n, 2)

        @pl.when(n >= 2)
        def _():
            arrived(piece)

        multiply(piece, 0, CHIPS)
        return carry

    lax.fori_loop(0, 4, near, 0)
    copies = []
    middle = CHIPS // 2
    for part in range(2):
        def far(n, carry):
            piece = (1 - half) * 4 + n
            if part == 0:
                arrived(piece)
            multiply(piece, part * middle, middle)
            return carry

        lax.fori_loop(0, 4, far, 0)
        span = slice(part * middle * 2 * MOST, (part + 1) * middle * 2 * MOST)
        gate = gate_sum[span]
        hidden[t, span] = (gate / (1.0 + jnp.exp(-gate)) * up_sum[span]).astype(BF16)
        for n, y in enumerate((across, above, below)):
            mine = hidden.at[t, span]
            copies.append(
                remote(mine, mine, hid_send.at[part, n], hid_recv.at[part, n], (index, y))
            )
            copies[-1].start()
    for copy in drops:
        copy.wait()
    found = term[t].astype(F32)
    for n in range(3):
        found = found + gained[n].astype(F32)
    slice_ref[...] = found.astype(BF16)
    gone = told.at[pl.ds(0, CHIPS - 1)]
    remote(gone, gone, told_send.at[0], told_recv.at[0], (mate, t)).wait_send()
    for c in range(2):
        gone = held.at[c, pl.ds(0, CHIPS - 1)]
        remote(gone, gone, held_send.at[c], held_recv.at[c, 0], (mate, t)).wait_send()
        whole = other.at[c]
        for sem in (sib_send, y_send, y_sib_send):
            remote(whole, whole, sem.at[c], rows_recv.at[0], (mate, t)).wait_send()
    for copy in copies:
        copy.wait()
    every_ref[...] = hidden[...]


def dispatch(tokens, told, gate_weight, up_weight, down, chosen):
    tok_rows, width = tokens.shape
    own = gate_weight.shape[2]
    wide = width // 8
    slots = CHIPS * 2 * MOST
    rows_own, width_out = down.shape
    count, share = chosen.shape[1], width_out // 4
    whole = pl.BlockSpec(memory_space=pltpu.VMEM)
    left = pl.BlockSpec(memory_space=pl.ANY)
    dma = pltpu.SemaphoreType.DMA
    return pl.pallas_call(
        dispatch_kernel,
        out_shape=[
            jax.ShapeDtypeStruct((4, slots, own), BF16),
            jax.ShapeDtypeStruct((count, share), BF16),
        ],
        in_specs=[left, whole, left, left, left, whole],
        out_specs=[whole, whole],
        scratch_shapes=[
            pltpu.VMEM((2, CHIPS, CORES * tok_rows, wide), BF16),
            pltpu.VMEM((CHIPS, CORES, 8, 128), jnp.int32),
            pltpu.VMEM((8, CHIPS, 2 * MOST, wide), BF16),
            pltpu.VMEM((2, CHIPS, 2 * MOST, wide), BF16),
            pltpu.VMEM((width, own), BF16),
            pltpu.VMEM((width, own), BF16),
            pltpu.VMEM((slots, own), F32),
            pltpu.VMEM((slots, own), F32),
            pltpu.VMEM((4, slots, own), BF16),
            dma((2,)), dma((2, CHIPS)), dma((1,)), dma((CHIPS,)), dma((8,)), dma((2,)), dma((2,)),
            dma((2,)), dma((3,)), dma((3,)), dma((3,)), dma((2,)), dma((2, 3)), dma((2, 3)),
            pltpu.VMEM((rows_own, width_out), BF16),
            pltpu.VMEM((4, count, share), BF16),
            pltpu.VMEM((3, count, share), BF16),
            dma((1,)), dma((3,)), dma((3,)),
        ],
        compiler_params=pltpu.CompilerParams(
            collective_id=0, has_side_effects=True, vmem_limit_bytes=48 * 2**20
        ),
        cost_estimate=pl.CostEstimate(
            flops=4 * slots * width * own, bytes_accessed=4 * width * own, transcendentals=slots * own
        ),
    )(tokens, told, gate_weight, up_weight, down, chosen)


def local(tokens, routes, gate_weight, up_weight, down_weight, removed):
    tok_rows, top = routes.shape
    down = down_weight[0]
    core = lax.rem(lax.axis_index("expert"), CORES)
    told = lax.dynamic_update_slice(
        jnp.full((top, 128), -1, jnp.int32), routes.T, (0, core * tok_rows)
    )
    every, part = dispatch(tokens, told, gate_weight, up_weight, down, removed)
    return solve(every, removed, down, part)[None]


def solution(mesh):
    in_specs = (
        P("expert", None),
        P("expert", None),
        P("expert", None, "tensor"),
        P("expert", None, "tensor"),
        P("expert", "tensor", None),
        P("expert", None),
    )
    out_specs = P("expert", "tensor", None)
    return jax.shard_map(local, mesh=mesh, in_specs=in_specs, out_specs=out_specs, check_vma=False)
```

```python
import jax
import jax.numpy as jnp
from jax import lax
from jax.experimental import pallas as pl
from jax.experimental.pallas import tpu as pltpu
from jax.sharding import PartitionSpec as P

DAMPING = 0.1
F32 = jnp.float32
BF16 = jnp.bfloat16
MESH = pl.DeviceIdType.MESH
SINGLE = 2
ROUNDS = 9
CAP = 1.85


def dot(a, b, left=1, right=0):
    return lax.dot_general(a, b, (((left,), (right,)), ((), ())), preferred_element_type=F32)


def split(x):
    high = x.astype(BF16)
    return high, (x - high.astype(F32)).astype(BF16)


def three(ah, al, bh, bl):
    return dot(ah, bh) + dot(ah, bl) + dot(al, bh)


def scales(lowest, rounds):
    out = []
    for _ in range(rounds):
        scale = min(2.0 / (1.0 + lowest), CAP)
        out.append(scale)
        lowest = 1.0 - (1.0 - scale * lowest) ** 2
    return out


def solve_kernel(
    every_ref, chosen_ref, down_ref, slice_ref, out_ref,
    down, dropped, result, load_sem, store_sem, send_sem, recv_sem,
):
    index = lax.axis_index("expert")
    me = lax.axis_index("tensor")
    load = pltpu.make_async_copy(down_ref, down, load_sem.at[0])
    load.start()
    others = [lax.rem(me + n, 4) for n in (1, 3, 2)]
    barrier = pltpu.get_barrier_semaphore()
    for y in others:
        pl.semaphore_signal(barrier, inc=1, device_id=(index, y), device_id_type=MESH)
    dropped[me] = slice_ref[...]
    pl.semaphore_wait(barrier, 3)
    copies = [
        pltpu.make_async_remote_copy(
            src_ref=slice_ref, dst_ref=dropped.at[me], send_sem=send_sem.at[n], recv_sem=recv_sem.at[n],
            device_id=(index, y), device_id_type=MESH,
        )
        for n, y in enumerate(others)
    ]
    for copy in copies:
        copy.start()
    parts, rows, own = every_ref.shape
    count = chosen_ref.shape[1]
    order = parts * own
    chosen = chosen_ref[...]
    total = jnp.zeros((1, 1), F32)
    removed = jnp.zeros((rows, count), F32)
    gram = jnp.zeros((rows, rows), F32)
    for part in range(parts):
        block = every_ref[part].astype(F32)
        total = total + jnp.sum(block * block, keepdims=True)
        units = lax.broadcasted_iota(jnp.int32, (own, count), 0) + part * own
        picks = (units == chosen).astype(F32).astype(BF16)
        removed = removed + dot(every_ref[part], picks)
        gone = dot(jnp.ones((8, count), BF16), picks, 1, 1)[:1]
        kept = (block * (1.0 - gone)).astype(BF16)
        gram = gram + dot(kept, kept, 1, 1)
    shift = total * (DAMPING / order) + 1e-6
    bound = total + shift
    inverse_bound = 1.0 / bound
    eye = (
        lax.broadcasted_iota(jnp.int32, (rows, rows), 0)
        == lax.broadcasted_iota(jnp.int32, (rows, rows), 1)
    ).astype(F32)
    gram = (gram + shift * eye) * inverse_bound
    lowest = 0.99 * (DAMPING / order) / (1.0 + DAMPING / order)
    steps = scales(lowest, ROUNDS)
    gh, gl = split(gram)
    x = 2.0 * steps[0] * eye - steps[0] ** 2 * gram
    for k in range(1, ROUNDS):
        scale = steps[k]
        if k <= SINGLE:
            xh = x.astype(BF16)
            z = dot(xh, dot(gh, xh).astype(BF16))
        else:
            xh, xl = split(x)
            yh, yl = split(three(gh, gl, xh, xl))
            z = three(xh, xl, yh, yl)
        x = 2.0 * scale * x - scale ** 2 * z
    xh, xl = split(x)
    rh = removed.astype(BF16)
    w = dot(xh, rh) + dot(xl, rh)
    wh, wl = split(w)
    rest = (removed - three(gh, gl, wh, wl)).astype(BF16)
    w = (w + dot(xh, rest)) * inverse_bound
    wh, wl = split(w)
    mine = every_ref[me]
    units = lax.broadcasted_iota(jnp.int32, (own, count), 0) + me * own
    keep = 1.0 - jnp.sum((units == chosen).astype(F32), axis=1, keepdims=True)
    mixing = (dot(mine, wh, 0, 0) + dot(mine, wl, 0, 0)) * keep
    high, low = split(mixing)
    load.wait()
    tile = dropped.shape[2]
    stores = []
    for n, quarter in enumerate((me, others[1], others[0], others[2])):
        if n:
            copies[n - 1].wait()
        at = pl.ds(pl.multiple_of(quarter * tile, 128), tile)
        part = dropped[quarter]
        change = dot(high, part) + dot(low, part)
        result[:, at] = ((down[:, at].astype(F32) + change) * keep).astype(BF16)
        stores.append(pltpu.make_async_copy(result.at[:, at], out_ref.at[:, at], store_sem.at[n]))
        stores[-1].start()
    for copy in stores:
        copy.wait()


def solve(every, chosen, down, part):
    own, width = down.shape
    count = chosen.shape[1]
    whole = pl.BlockSpec(memory_space=pltpu.VMEM)
    left = pl.BlockSpec(memory_space=pl.ANY)
    return pl.pallas_call(
        solve_kernel,
        out_shape=jax.ShapeDtypeStruct((own, width), BF16),
        in_specs=[whole, whole, left, whole],
        out_specs=left,
        scratch_shapes=[
            pltpu.VMEM((own, width), BF16),
            pltpu.VMEM((4, count, width // 4), BF16),
            pltpu.VMEM((own, width), BF16),
            pltpu.SemaphoreType.DMA((1,)),
            pltpu.SemaphoreType.DMA((4,)),
            pltpu.SemaphoreType.DMA((3,)),
            pltpu.SemaphoreType.DMA((3,)),
        ],
        compiler_params=pltpu.CompilerParams(
            collective_id=1, has_side_effects=True, vmem_limit_bytes=48 * 2**20
        ),
    )(every, chosen, down, part)


ZS, XS = 8, 4
CHIPS = ZS * XS
CORES = 2
MOST = 8


def dispatch_kernel(
    tok_ref, route_ref, gate_ref, up_ref, down_ref, chosen_ref, every_ref, slice_ref,
    held, told, rows, other, gate_w, up_w, gate_sum, up_sum, hidden,
    held_send, held_recv, told_send, told_recv, rows_recv, sib_send, y_send, y_sib_send,
    pre_send, pre_recv, local_sem, weight_sem, hid_send, hid_recv,
    down, term, gained, down_sem, drop_send, drop_recv,
):
    index = lax.axis_index("expert")
    t = lax.axis_index("tensor")
    core = lax.rem(index, 2)
    chip = index // 2
    z, x = chip // XS, lax.rem(chip, XS)
    half = lax.rem(t, 2)
    mate = chip * 2 + 1 - core
    above, below, across = lax.rem(t + 1, 4), lax.rem(t + 3, 4), lax.rem(t + 2, 4)
    here = chip
    z_up, z_down = (lax.rem(z + 1, ZS) * XS + x) * 2 + core, (lax.rem(z + ZS - 1, ZS) * XS + x) * 2 + core
    x_up, x_down = (z * XS + lax.rem(x + 1, XS)) * 2 + core, (z * XS + lax.rem(x + XS - 1, XS)) * 2 + core
    tok_rows = tok_ref.shape[0]
    wide = held.shape[-1]

    loads = [
        pltpu.make_async_copy(gate_ref.at[0], gate_w, weight_sem.at[0]),
        pltpu.make_async_copy(up_ref.at[0], up_w, weight_sem.at[1]),
    ]
    down_load = pltpu.make_async_copy(down_ref, down, down_sem.at[0])
    down_load.start()

    barrier = pltpu.get_barrier_semaphore()
    partners = [(n, t) for n in (z_up, z_down, x_up, x_down)] + [(mate, t)]
    partners += [(e, y) for e in (index, mate) for y in (above, below)] + [(index, across)]
    for partner in partners:
        pl.semaphore_signal(barrier, inc=1, device_id=partner, device_id_type=MESH)
    pl.semaphore_wait(barrier, len(partners))

    def remote(src, dst, send, recv, to):
        return pltpu.make_async_remote_copy(
            src_ref=src, dst_ref=dst, send_sem=send, recv_sem=recv, device_id=to, device_id_type=MESH
        )

    def columns(of_core, cycle):
        first = half * (4 * wide) + of_core * (2 * wide) + cycle * wide
        return pl.ds(pl.multiple_of(first, 128), wide)

    band = pl.ds(pl.multiple_of(core * tok_rows, 32), tok_rows)
    first = []
    for c in range(2):
        first.append(
            remote(
                tok_ref.at[:, columns(1 - core, c)], held.at[c, here, band],
                pre_send.at[c], pre_recv.at[c], (mate, t),
            )
        )
    first.append(
        remote(route_ref, told.at[here, core], pre_send.at[2], pre_recv.at[2], (mate, t))
    )
    for copy in first:
        copy.start()
    own = []
    for c in range(2):
        own.append(
            pltpu.make_async_copy(
                tok_ref.at[:, columns(core, c)], held.at[c, here, band], local_sem.at[c]
            )
        )
    own.append(pltpu.make_async_copy(route_ref, told.at[here, core], local_sem.at[2]))
    for copy in own + loads:
        copy.start()
    for copy in own:
        copy.wait()
    for copy in first:
        copy.wait()

    def at(dz, dx):
        return lax.rem(z + dz + 2 * ZS, ZS) * XS + lax.rem(x + dx + 2 * XS, XS)

    def go(c, block, to):
        remote(
            held.at[c, block], held.at[c, block], held_send.at[c], held_recv.at[c, block], (to, t)
        ).start()
        if c == 0:
            remote(
                told.at[block], told.at[block], told_send.at[0], told_recv.at[block], (to, t)
            ).start()

    def take(c, block):
        remote(
            held.at[c, block], held.at[c, block], held_send.at[c], held_recv.at[c, block], (mate, t)
        ).wait_recv()
        if c == 0:
            remote(
                told.at[block], told.at[block], told_send.at[0], told_recv.at[block], (mate, t)
            ).wait_recv()

    lane = lax.broadcasted_iota(jnp.int32, (128, 128), 1)
    earlier = (lax.broadcasted_iota(jnp.int32, (128, 128), 0) < lane).astype(F32).astype(BF16)
    slot = lax.rem(lax.broadcasted_iota(jnp.int32, (4 * MOST, 128), 0), MOST).astype(F32)

    def pick(events):
        marks = []
        for c, block in events:
            for expert in (index, mate):
                for h in range(CORES):
                    named = (told[block, h] == expert).astype(F32)
                    marks.append(jnp.broadcast_to(jnp.sum(named, axis=0, keepdims=True), (MOST, 128)))
        marks = jnp.concatenate(marks, axis=0)
        ranks = dot(marks.astype(BF16), earlier)
        out = []
        for n, (c, block) in enumerate(events):
            part = slice(n * 4 * MOST, (n + 1) * 4 * MOST)
            hits = jnp.where(ranks[part] == slot, marks[part], 0.0)[:, : CORES * tok_rows]
            out.append(dot(hits.astype(BF16), held[c, block]).astype(BF16))
        for (c, source), picked in zip(events, out):
            rows[half * 4 + core * 2 + c, source] = picked[: 2 * MOST]
            other[c, source] = picked[2 * MOST :]
        for c, source in events:
            piece = half * 4 + core * 2 + c
            y = above if c == 0 else below
            target = rows.at[piece, source]
            got = rows_recv.at[piece]
            remote(other.at[c, source], target, y_sib_send.at[c], got, (mate, y)).start()
            remote(rows.at[piece, source], target, y_send.at[c], got, (index, y)).start()
            remote(other.at[c, source], target, sib_send.at[c], got, (mate, t)).start()

    for c in range(2):
        for to in (z_up, z_down, x_up, x_down):
            go(c, here, to)
    pick([(0, here), (1, here)])

    down_load.wait()
    own_rows, count = down.shape[0], chosen_ref.shape[1]
    units = lax.broadcasted_iota(jnp.int32, (own_rows, count), 0) + t * own_rows
    picks = (units == chosen_ref[...]).astype(F32).astype(BF16)
    share = term.shape[-1]
    for u in range(4):
        term[u] = dot(picks, down[:, u * share : (u + 1) * share], 0, 0).astype(BF16)
    drops = [
        remote(term.at[y], gained.at[n], drop_send.at[n], drop_recv.at[n], (index, y))
        for n, y in enumerate((across, above, below))
    ]
    for copy in drops:
        copy.start()

    def turn(r, carry):
        @pl.when(r <= 4)
        def _():
            block = at(-r, 0)
            take(0, block)

            @pl.when(r < 4)
            def _():
                go(0, block, z_up)

            go(0, block, x_up)
            go(0, block, x_down)

        @pl.when(r <= 3)
        def _():
            block = at(r, 0)
            take(0, block)

            @pl.when(r < 3)
            def _():
                go(0, block, z_down)

            go(0, block, x_up)
            go(0, block, x_down)

        @pl.when(r == 1)
        def _():
            block = at(0, -1)
            take(1, block)
            go(1, block, x_up)
            go(1, block, z_up)
            go(1, block, z_down)
            block = at(0, 1)
            take(1, block)
            go(1, block, z_up)
            go(1, block, z_down)

        @pl.when(r == 2)
        def _():
            block = at(0, 2)
            take(1, block)
            go(1, block, z_up)
            go(1, block, z_down)

        for dx in (0, -1, 1, 2):
            hop = r - abs(dx)
            even = lax.rem(x + dx + XS, 2) == 0
            for sign, to, most in ((-1, z_up, jnp.where(even, 4, 3)), (1, z_down, jnp.where(even, 3, 4))):
                @pl.when((hop >= 1) & (hop <= most))
                def _():
                    block = at(sign * hop, dx)
                    take(1, block)

                    @pl.when(hop < most)
                    def _():
                        go(1, block, to)

        for sign in (-1, 1):
            far = r - 1
            there = (far <= 4) if sign < 0 else (far >= 1) & (far <= 3)

            @pl.when(there)
            def _():
                even = lax.rem(z + far, 2) == 0
                block = at(sign * far, -1)
                take(0, block)

                @pl.when(even)
                def _():
                    go(0, block, x_up)

                back = at(sign * far, 1)
                take(0, back)

                @pl.when(jnp.logical_not(even))
                def _():
                    go(0, back, x_down)

        for sign in (-1, 1):
            far = r - 2
            there = (far >= 0) if sign < 0 else (far >= 1) & (far <= 3)

            @pl.when(there)
            def _():
                take(0, at(sign * far, 2))

        for dx in (0, -1, 1, 2):
            far = r - abs(dx)
            for sign in (-1, 1):
                there = (far >= 0) & (far <= 4) if sign < 0 else (far >= 1) & (far <= 3)

                @pl.when(there)
                def _():
                    block = at(sign * far, dx)
                    pick([(0, block), (1, block)])

        return carry

    lax.fori_loop(1, 7, turn, 0)

    for load in loads:
        load.wait()
    gate_sum[...] = jnp.zeros_like(gate_sum)
    up_sum[...] = jnp.zeros_like(up_sum)

    def multiply(piece, first, count):
        cut = pl.ds(pl.multiple_of(piece * wide, 128), wide)
        block = rows[piece, first : first + count].reshape(count * 2 * MOST, wide)
        span = slice(first * 2 * MOST, (first + count) * 2 * MOST)
        gate_sum[span] += dot(block, gate_w[cut, :])
        up_sum[span] += dot(block, up_w[cut, :])

    def arrived(piece):
        remote(
            rows.at[piece], rows.at[piece], sib_send.at[0], rows_recv.at[piece], (mate, t)
        ).wait_recv()

    def near(n, carry):
        piece = half * 4 + jnp.where(n < 2, core, 1 - core) * 2 + lax.rem(n, 2)

        @pl.when(n >= 2)
        def _():
            arrived(piece)

        multiply(piece, 0, CHIPS)
        return carry

    lax.fori_loop(0, 4, near, 0)
    copies = []
    middle = CHIPS // 2
    for part in range(2):
        def far(n, carry):
            piece = (1 - half) * 4 + n
            if part == 0:
                arrived(piece)
            multiply(piece, part * middle, middle)
            return carry

        lax.fori_loop(0, 4, far, 0)
        span = slice(part * middle * 2 * MOST, (part + 1) * middle * 2 * MOST)
        gate = gate_sum[span]
        hidden[t, span] = (gate / (1.0 + jnp.exp(-gate)) * up_sum[span]).astype(BF16)
        for n, y in enumerate((across, above, below)):
            mine = hidden.at[t, span]
            copies.append(
                remote(mine, mine, hid_send.at[part, n], hid_recv.at[part, n], (index, y))
            )
            copies[-1].start()
    for copy in drops:
        copy.wait()
    found = term[t].astype(F32)
    for n in range(3):
        found = found + gained[n].astype(F32)
    slice_ref[...] = found.astype(BF16)
    gone = told.at[pl.ds(0, CHIPS - 1)]
    remote(gone, gone, told_send.at[0], told_recv.at[0], (mate, t)).wait_send()
    for c in range(2):
        gone = held.at[c, pl.ds(0, CHIPS - 1)]
        remote(gone, gone, held_send.at[c], held_recv.at[c, 0], (mate, t)).wait_send()
        whole = other.at[c]
        for sem in (sib_send, y_send, y_sib_send):
            remote(whole, whole, sem.at[c], rows_recv.at[0], (mate, t)).wait_send()
    for copy in copies:
        copy.wait()
    every_ref[...] = hidden[...]


def dispatch(tokens, told, gate_weight, up_weight, down, chosen):
    tok_rows, width = tokens.shape
    own = gate_weight.shape[2]
    wide = width // 8
    slots = CHIPS * 2 * MOST
    rows_own, width_out = down.shape
    count, share = chosen.shape[1], width_out // 4
    whole = pl.BlockSpec(memory_space=pltpu.VMEM)
    left = pl.BlockSpec(memory_space=pl.ANY)
    dma = pltpu.SemaphoreType.DMA
    return pl.pallas_call(
        dispatch_kernel,
        out_shape=[
            jax.ShapeDtypeStruct((4, slots, own), BF16),
            jax.ShapeDtypeStruct((count, share), BF16),
        ],
        in_specs=[left, whole, left, left, left, whole],
        out_specs=[whole, whole],
        scratch_shapes=[
            pltpu.VMEM((2, CHIPS, CORES * tok_rows, wide), BF16),
            pltpu.VMEM((CHIPS, CORES, 8, 128), jnp.int32),
            pltpu.VMEM((8, CHIPS, 2 * MOST, wide), BF16),
            pltpu.VMEM((2, CHIPS, 2 * MOST, wide), BF16),
            pltpu.VMEM((width, own), BF16),
            pltpu.VMEM((width, own), BF16),
            pltpu.VMEM((slots, own), F32),
            pltpu.VMEM((slots, own), F32),
            pltpu.VMEM((4, slots, own), BF16),
            dma((2,)), dma((2, CHIPS)), dma((1,)), dma((CHIPS,)), dma((8,)), dma((2,)), dma((2,)),
            dma((2,)), dma((3,)), dma((3,)), dma((3,)), dma((2,)), dma((2, 3)), dma((2, 3)),
            pltpu.VMEM((rows_own, width_out), BF16),
            pltpu.VMEM((4, count, share), BF16),
            pltpu.VMEM((3, count, share), BF16),
            dma((1,)), dma((3,)), dma((3,)),
        ],
        compiler_params=pltpu.CompilerParams(
            collective_id=0, has_side_effects=True, vmem_limit_bytes=48 * 2**20
        ),
        cost_estimate=pl.CostEstimate(
            flops=4 * slots * width * own, bytes_accessed=4 * width * own, transcendentals=slots * own
        ),
    )(tokens, told, gate_weight, up_weight, down, chosen)


def local(tokens, routes, gate_weight, up_weight, down_weight, removed):
    tok_rows, top = routes.shape
    down = down_weight[0]
    core = lax.rem(lax.axis_index("expert"), CORES)
    told = lax.dynamic_update_slice(
        jnp.full((top, 128), -1, jnp.int32), routes.T, (0, core * tok_rows)
    )
    every, part = dispatch(tokens, told, gate_weight, up_weight, down, removed)
    return solve(every, removed, down, part)[None]


def solution(mesh):
    in_specs = (
        P("expert", None),
        P("expert", None),
        P("expert", None, "tensor"),
        P("expert", None, "tensor"),
        P("expert", "tensor", None),
        P("expert", None),
    )
    out_specs = P("expert", "tensor", None)
    return jax.shard_map(local, mesh=mesh, in_specs=in_specs, out_specs=out_specs, check_vma=False)
```

```python
import jax
import jax.numpy as jnp
from jax import lax
from jax.experimental import pallas as pl
from jax.experimental.pallas import tpu as pltpu
from jax.sharding import PartitionSpec as P

DAMPING = 0.1
F32 = jnp.float32
BF16 = jnp.bfloat16
MESH = pl.DeviceIdType.MESH
SINGLE = 2
ROUNDS = 9
CAP = 1.85


def dot(a, b, left=1, right=0):
    return lax.dot_general(a, b, (((left,), (right,)), ((), ())), preferred_element_type=F32)


def split(x):
    high = x.astype(BF16)
    return high, (x - high.astype(F32)).astype(BF16)


def three(ah, al, bh, bl):
    return dot(ah, bh) + dot(ah, bl) + dot(al, bh)


def scales(lowest, rounds):
    out = []
    for _ in range(rounds):
        scale = min(2.0 / (1.0 + lowest), CAP)
        out.append(scale)
        lowest = 1.0 - (1.0 - scale * lowest) ** 2
    return out


def solve_kernel(
    every_ref, chosen_ref, down_ref, slice_ref, out_ref,
    down, dropped, result, load_sem, store_sem, send_sem, recv_sem,
):
    index = lax.axis_index("expert")
    me = lax.axis_index("tensor")
    load = pltpu.make_async_copy(down_ref, down, load_sem.at[0])
    load.start()
    others = [lax.rem(me + n, 4) for n in (1, 3, 2)]
    barrier = pltpu.get_barrier_semaphore()
    for y in others:
        pl.semaphore_signal(barrier, inc=1, device_id=(index, y), device_id_type=MESH)
    dropped[me] = slice_ref[...]
    pl.semaphore_wait(barrier, 3)
    copies = [
        pltpu.make_async_remote_copy(
            src_ref=slice_ref, dst_ref=dropped.at[me], send_sem=send_sem.at[n], recv_sem=recv_sem.at[n],
            device_id=(index, y), device_id_type=MESH,
        )
        for n, y in enumerate(others)
    ]
    for copy in copies:
        copy.start()
    parts, rows, own = every_ref.shape
    count = chosen_ref.shape[1]
    order = parts * own
    chosen = chosen_ref[...]
    total = jnp.zeros((1, 1), F32)
    removed = jnp.zeros((rows, count), F32)
    gram = jnp.zeros((rows, rows), F32)
    for part in range(parts):
        block = every_ref[part].astype(F32)
        total = total + jnp.sum(block * block, keepdims=True)
        units = lax.broadcasted_iota(jnp.int32, (own, count), 0) + part * own
        picks = (units == chosen).astype(F32).astype(BF16)
        removed = removed + dot(every_ref[part], picks)
        gone = dot(jnp.ones((8, count), BF16), picks, 1, 1)[:1]
        kept = (block * (1.0 - gone)).astype(BF16)
        gram = gram + dot(kept, kept, 1, 1)
    shift = total * (DAMPING / order) + 1e-6
    bound = total + shift
    inverse_bound = 1.0 / bound
    eye = (
        lax.broadcasted_iota(jnp.int32, (rows, rows), 0)
        == lax.broadcasted_iota(jnp.int32, (rows, rows), 1)
    ).astype(F32)
    gram = (gram + shift * eye) * inverse_bound
    lowest = 0.99 * (DAMPING / order) / (1.0 + DAMPING / order)
    steps = scales(lowest, ROUNDS)
    gh, gl = split(gram)
    x = 2.0 * steps[0] * eye - steps[0] ** 2 * gram
    for k in range(1, ROUNDS):
        scale = steps[k]
        if k <= SINGLE:
            xh = x.astype(BF16)
            z = dot(xh, dot(gh, xh).astype(BF16))
        else:
            xh, xl = split(x)
            yh, yl = split(three(gh, gl, xh, xl))
            z = three(xh, xl, yh, yl)
        x = 2.0 * scale * x - scale ** 2 * z
    xh, xl = split(x)
    rh = removed.astype(BF16)
    w = dot(xh, rh) + dot(xl, rh)
    wh, wl = split(w)
    rest = (removed - three(gh, gl, wh, wl)).astype(BF16)
    w = (w + dot(xh, rest)) * inverse_bound
    wh, wl = split(w)
    mine = every_ref[me]
    units = lax.broadcasted_iota(jnp.int32, (own, count), 0) + me * own
    keep = 1.0 - jnp.sum((units == chosen).astype(F32), axis=1, keepdims=True)
    mixing = (dot(mine, wh, 0, 0) + dot(mine, wl, 0, 0)) * keep
    high, low = split(mixing)
    load.wait()
    tile = dropped.shape[2]
    stores = []
    for n, quarter in enumerate((me, others[1], others[0], others[2])):
        if n:
            copies[n - 1].wait()
        at = pl.ds(pl.multiple_of(quarter * tile, 128), tile)
        part = dropped[quarter]
        change = dot(high, part) + dot(low, part)
        result[:, at] = ((down[:, at].astype(F32) + change) * keep).astype(BF16)
        stores.append(pltpu.make_async_copy(result.at[:, at], out_ref.at[:, at], store_sem.at[n]))
        stores[-1].start()
    for copy in stores:
        copy.wait()


def solve(every, chosen, down, part):
    own, width = down.shape
    count = chosen.shape[1]
    whole = pl.BlockSpec(memory_space=pltpu.VMEM)
    left = pl.BlockSpec(memory_space=pl.ANY)
    return pl.pallas_call(
        solve_kernel,
        out_shape=jax.ShapeDtypeStruct((own, width), BF16),
        in_specs=[whole, whole, left, whole],
        out_specs=left,
        scratch_shapes=[
            pltpu.VMEM((own, width), BF16),
            pltpu.VMEM((4, count, width // 4), BF16),
            pltpu.VMEM((own, width), BF16),
            pltpu.SemaphoreType.DMA((1,)),
            pltpu.SemaphoreType.DMA((4,)),
            pltpu.SemaphoreType.DMA((3,)),
            pltpu.SemaphoreType.DMA((3,)),
        ],
        compiler_params=pltpu.CompilerParams(
            collective_id=1, has_side_effects=True, vmem_limit_bytes=48 * 2**20
        ),
    )(every, chosen, down, part)


ZS, XS = 8, 4
CHIPS = ZS * XS
CORES = 2
MOST = 8


def dispatch_kernel(
    tok_ref, route_ref, gate_ref, up_ref, down_ref, chosen_ref, every_ref, slice_ref,
    held, told, rows, other, gate_w, up_w, gate_sum, up_sum, hidden,
    held_send, held_recv, told_send, told_recv, rows_recv, sib_send, y_send, y_sib_send,
    pre_send, pre_recv, local_sem, weight_sem, hid_send, hid_recv,
    down, term, gained, down_sem, drop_send, drop_recv,
):
    index = lax.axis_index("expert")
    t = lax.axis_index("tensor")
    core = lax.rem(index, 2)
    chip = index // 2
    z, x = chip // XS, lax.rem(chip, XS)
    half = lax.rem(t, 2)
    mate = chip * 2 + 1 - core
    above, below, across = lax.rem(t + 1, 4), lax.rem(t + 3, 4), lax.rem(t + 2, 4)
    here = chip
    z_up, z_down = (lax.rem(z + 1, ZS) * XS + x) * 2 + core, (lax.rem(z + ZS - 1, ZS) * XS + x) * 2 + core
    x_up, x_down = (z * XS + lax.rem(x + 1, XS)) * 2 + core, (z * XS + lax.rem(x + XS - 1, XS)) * 2 + core
    tok_rows = tok_ref.shape[0]
    wide = held.shape[-1]

    loads = [
        pltpu.make_async_copy(gate_ref.at[0], gate_w, weight_sem.at[0]),
        pltpu.make_async_copy(up_ref.at[0], up_w, weight_sem.at[1]),
    ]
    down_load = pltpu.make_async_copy(down_ref, down, down_sem.at[0])
    down_load.start()

    barrier = pltpu.get_barrier_semaphore()
    partners = [(n, t) for n in (z_up, z_down, x_up, x_down)] + [(mate, t)]
    partners += [(e, y) for e in (index, mate) for y in (above, below)] + [(index, across)]
    for partner in partners:
        pl.semaphore_signal(barrier, inc=1, device_id=partner, device_id_type=MESH)
    pl.semaphore_wait(barrier, len(partners))

    def remote(src, dst, send, recv, to):
        return pltpu.make_async_remote_copy(
            src_ref=src, dst_ref=dst, send_sem=send, recv_sem=recv, device_id=to, device_id_type=MESH
        )

    def columns(of_core, cycle):
        first = half * (4 * wide) + of_core * (2 * wide) + cycle * wide
        return pl.ds(pl.multiple_of(first, 128), wide)

    band = pl.ds(pl.multiple_of(core * tok_rows, 32), tok_rows)
    first = []
    for c in range(2):
        first.append(
            remote(
                tok_ref.at[:, columns(1 - core, c)], held.at[c, here, band],
                pre_send.at[c], pre_recv.at[c], (mate, t),
            )
        )
    first.append(
        remote(route_ref, told.at[here, core], pre_send.at[2], pre_recv.at[2], (mate, t))
    )
    for copy in first:
        copy.start()
    own = []
    for c in range(2):
        own.append(
            pltpu.make_async_copy(
                tok_ref.at[:, columns(core, c)], held.at[c, here, band], local_sem.at[c]
            )
        )
    own.append(pltpu.make_async_copy(route_ref, told.at[here, core], local_sem.at[2]))
    for copy in own + loads:
        copy.start()
    down_load.wait()
    own_rows, count = down.shape[0], chosen_ref.shape[1]
    units = lax.broadcasted_iota(jnp.int32, (own_rows, count), 0) + t * own_rows
    picks = (units == chosen_ref[...]).astype(F32).astype(BF16)
    share = term.shape[-1]
    for u in range(4):
        term[u] = dot(picks, down[:, u * share : (u + 1) * share], 0, 0).astype(BF16)
    drops = [
        remote(term.at[y], gained.at[n], drop_send.at[n], drop_recv.at[n], (index, y))
        for n, y in enumerate((across, above, below))
    ]
    for copy in drops:
        copy.start()

    for copy in own:
        copy.wait()
    for copy in first:
        copy.wait()

    def at(dz, dx):
        return lax.rem(z + dz + 2 * ZS, ZS) * XS + lax.rem(x + dx + 2 * XS, XS)

    def go(c, block, to):
        remote(
            held.at[c, block], held.at[c, block], held_send.at[c], held_recv.at[c, block], (to, t)
        ).start()
        if c == 0:
            remote(
                told.at[block], told.at[block], told_send.at[0], told_recv.at[block], (to, t)
            ).start()

    def take(c, block):
        remote(
            held.at[c, block], held.at[c, block], held_send.at[c], held_recv.at[c, block], (mate, t)
        ).wait_recv()
        if c == 0:
            remote(
                told.at[block], told.at[block], told_send.at[0], told_recv.at[block], (mate, t)
            ).wait_recv()

    lane = lax.broadcasted_iota(jnp.int32, (128, 128), 1)
    earlier = (lax.broadcasted_iota(jnp.int32, (128, 128), 0) < lane).astype(F32).astype(BF16)
    slot = lax.rem(lax.broadcasted_iota(jnp.int32, (4 * MOST, 128), 0), MOST).astype(F32)

    def pick(events):
        marks = []
        for c, block in events:
            for expert in (index, mate):
                for h in range(CORES):
                    named = (told[block, h] == expert).astype(F32)
                    marks.append(jnp.broadcast_to(jnp.sum(named, axis=0, keepdims=True), (MOST, 128)))
        marks = jnp.concatenate(marks, axis=0)
        ranks = dot(marks.astype(BF16), earlier)
        out = []
        for n, (c, block) in enumerate(events):
            part = slice(n * 4 * MOST, (n + 1) * 4 * MOST)
            hits = jnp.where(ranks[part] == slot, marks[part], 0.0)[:, : CORES * tok_rows]
            out.append(dot(hits.astype(BF16), held[c, block]).astype(BF16))
        for (c, source), picked in zip(events, out):
            rows[half * 4 + core * 2 + c, source] = picked[: 2 * MOST]
            other[c, source] = picked[2 * MOST :]
        for c, source in events:
            piece = half * 4 + core * 2 + c
            y = above if c == 0 else below
            target = rows.at[piece, source]
            got = rows_recv.at[piece]
            remote(other.at[c, source], target, y_sib_send.at[c], got, (mate, y)).start()
            remote(rows.at[piece, source], target, y_send.at[c], got, (index, y)).start()
            remote(other.at[c, source], target, sib_send.at[c], got, (mate, t)).start()

    for c in range(2):
        for to in (z_up, z_down, x_up, x_down):
            go(c, here, to)
    pick([(0, here), (1, here)])

    def turn(r, carry):
        @pl.when(r <= 4)
        def _():
            block = at(-r, 0)
            take(0, block)

            @pl.when(r < 4)
            def _():
                go(0, block, z_up)

            go(0, block, x_up)
            go(0, block, x_down)

        @pl.when(r <= 3)
        def _():
            block = at(r, 0)
            take(0, block)

            @pl.when(r < 3)
            def _():
                go(0, block, z_down)

            go(0, block, x_up)
            go(0, block, x_down)

        @pl.when(r == 1)
        def _():
            block = at(0, -1)
            take(1, block)
            go(1, block, x_up)
            go(1, block, z_up)
            go(1, block, z_down)
            block = at(0, 1)
            take(1, block)
            go(1, block, z_up)
            go(1, block, z_down)

        @pl.when(r == 2)
        def _():
            block = at(0, 2)
            take(1, block)
            go(1, block, z_up)
            go(1, block, z_down)

        for dx in (0, -1, 1, 2):
            hop = r - abs(dx)
            even = lax.rem(x + dx + XS, 2) == 0
            for sign, to, most in ((-1, z_up, jnp.where(even, 4, 3)), (1, z_down, jnp.where(even, 3, 4))):
                @pl.when((hop >= 1) & (hop <= most))
                def _():
                    block = at(sign * hop, dx)
                    take(1, block)

                    @pl.when(hop < most)
                    def _():
                        go(1, block, to)

        for sign in (-1, 1):
            far = r - 1
            there = (far <= 4) if sign < 0 else (far >= 1) & (far <= 3)

            @pl.when(there)
            def _():
                even = lax.rem(z + far, 2) == 0
                block = at(sign * far, -1)
                take(0, block)

                @pl.when(even)
                def _():
                    go(0, block, x_up)

                back = at(sign * far, 1)
                take(0, back)

                @pl.when(jnp.logical_not(even))
                def _():
                    go(0, back, x_down)

        for sign in (-1, 1):
            far = r - 2
            there = (far >= 0) if sign < 0 else (far >= 1) & (far <= 3)

            @pl.when(there)
            def _():
                take(0, at(sign * far, 2))

        for dx in (0, -1, 1, 2):
            far = r - abs(dx)
            for sign in (-1, 1):
                there = (far >= 0) & (far <= 4) if sign < 0 else (far >= 1) & (far <= 3)

                @pl.when(there)
                def _():
                    block = at(sign * far, dx)
                    pick([(0, block), (1, block)])

        return carry

    lax.fori_loop(1, 7, turn, 0)

    for load in loads:
        load.wait()
    gate_sum[...] = jnp.zeros_like(gate_sum)
    up_sum[...] = jnp.zeros_like(up_sum)

    def multiply(piece, first, count):
        cut = pl.ds(pl.multiple_of(piece * wide, 128), wide)
        block = rows[piece, first : first + count].reshape(count * 2 * MOST, wide)
        span = slice(first * 2 * MOST, (first + count) * 2 * MOST)
        gate_sum[span] += dot(block, gate_w[cut, :])
        up_sum[span] += dot(block, up_w[cut, :])

    def arrived(piece):
        remote(
            rows.at[piece], rows.at[piece], sib_send.at[0], rows_recv.at[piece], (mate, t)
        ).wait_recv()

    def near(n, carry):
        piece = half * 4 + jnp.where(n < 2, core, 1 - core) * 2 + lax.rem(n, 2)

        @pl.when(n >= 2)
        def _():
            arrived(piece)

        multiply(piece, 0, CHIPS)
        return carry

    lax.fori_loop(0, 4, near, 0)
    copies = []
    middle = CHIPS // 2
    for part in range(2):
        def far(n, carry):
            piece = (1 - half) * 4 + n
            if part == 0:
                arrived(piece)
            multiply(piece, part * middle, middle)
            return carry

        lax.fori_loop(0, 4, far, 0)
        span = slice(part * middle * 2 * MOST, (part + 1) * middle * 2 * MOST)
        gate = gate_sum[span]
        hidden[t, span] = (gate / (1.0 + jnp.exp(-gate)) * up_sum[span]).astype(BF16)
        for n, y in enumerate((across, above, below)):
            mine = hidden.at[t, span]
            copies.append(
                remote(mine, mine, hid_send.at[part, n], hid_recv.at[part, n], (index, y))
            )
            copies[-1].start()
    for copy in drops:
        copy.wait()
    found = term[t].astype(F32)
    for n in range(3):
        found = found + gained[n].astype(F32)
    slice_ref[...] = found.astype(BF16)
    gone = told.at[pl.ds(0, CHIPS - 1)]
    remote(gone, gone, told_send.at[0], told_recv.at[0], (mate, t)).wait_send()
    for c in range(2):
        gone = held.at[c, pl.ds(0, CHIPS - 1)]
        remote(gone, gone, held_send.at[c], held_recv.at[c, 0], (mate, t)).wait_send()
        whole = other.at[c]
        for sem in (sib_send, y_send, y_sib_send):
            remote(whole, whole, sem.at[c], rows_recv.at[0], (mate, t)).wait_send()
    for copy in copies:
        copy.wait()
    every_ref[...] = hidden[...]


def dispatch(tokens, told, gate_weight, up_weight, down, chosen):
    tok_rows, width = tokens.shape
    own = gate_weight.shape[2]
    wide = width // 8
    slots = CHIPS * 2 * MOST
    rows_own, width_out = down.shape
    count, share = chosen.shape[1], width_out // 4
    whole = pl.BlockSpec(memory_space=pltpu.VMEM)
    left = pl.BlockSpec(memory_space=pl.ANY)
    dma = pltpu.SemaphoreType.DMA
    return pl.pallas_call(
        dispatch_kernel,
        out_shape=[
            jax.ShapeDtypeStruct((4, slots, own), BF16),
            jax.ShapeDtypeStruct((count, share), BF16),
        ],
        in_specs=[left, whole, left, left, left, whole],
        out_specs=[whole, whole],
        scratch_shapes=[
            pltpu.VMEM((2, CHIPS, CORES * tok_rows, wide), BF16),
            pltpu.VMEM((CHIPS, CORES, 8, 128), jnp.int32),
            pltpu.VMEM((8, CHIPS, 2 * MOST, wide), BF16),
            pltpu.VMEM((2, CHIPS, 2 * MOST, wide), BF16),
            pltpu.VMEM((width, own), BF16),
            pltpu.VMEM((width, own), BF16),
            pltpu.VMEM((slots, own), F32),
            pltpu.VMEM((slots, own), F32),
            pltpu.VMEM((4, slots, own), BF16),
            dma((2,)), dma((2, CHIPS)), dma((1,)), dma((CHIPS,)), dma((8,)), dma((2,)), dma((2,)),
            dma((2,)), dma((3,)), dma((3,)), dma((3,)), dma((2,)), dma((2, 3)), dma((2, 3)),
            pltpu.VMEM((rows_own, width_out), BF16),
            pltpu.VMEM((4, count, share), BF16),
            pltpu.VMEM((3, count, share), BF16),
            dma((1,)), dma((3,)), dma((3,)),
        ],
        compiler_params=pltpu.CompilerParams(
            collective_id=0, has_side_effects=True, vmem_limit_bytes=48 * 2**20
        ),
        cost_estimate=pl.CostEstimate(
            flops=4 * slots * width * own, bytes_accessed=4 * width * own, transcendentals=slots * own
        ),
    )(tokens, told, gate_weight, up_weight, down, chosen)


def local(tokens, routes, gate_weight, up_weight, down_weight, removed):
    tok_rows, top = routes.shape
    down = down_weight[0]
    core = lax.rem(lax.axis_index("expert"), CORES)
    told = lax.dynamic_update_slice(
        jnp.full((top, 128), -1, jnp.int32), routes.T, (0, core * tok_rows)
    )
    every, part = dispatch(tokens, told, gate_weight, up_weight, down, removed)
    return solve(every, removed, down, part)[None]


def solution(mesh):
    in_specs = (
        P("expert", None),
        P("expert", None),
        P("expert", None, "tensor"),
        P("expert", None, "tensor"),
        P("expert", "tensor", None),
        P("expert", None),
    )
    out_specs = P("expert", "tensor", None)
    return jax.shard_map(local, mesh=mesh, in_specs=in_specs, out_specs=out_specs, check_vma=False)
```
